128 devices in a mesh: ch: 4 (over x_hi, core), tile: 32 (over y, x_lo, z).
Axes of the slice: x: 4 (x_hi: 2, x_lo: 2; x = x_hi * 2 + x_lo), y: 4, z: 4, core: 2. Of those that a mesh axis runs over, the one named last changes fastest.
Arguments:
- latent: bfloat16 [2, 8, 32, 8, 30, 512], P(None, None, 'tile', None, None, 'ch'), may hold values from -6 to 6
- expand_weight: bfloat16 [512, 2, 2048], P('tile', None, 'ch'), may hold values from -0.25 to 0.25
- depth_kernel: float32 [3, 3, 3, 2, 2048], P(None, None, None, None, 'ch'), may hold values from -1.25 to 1.25
- project_weight: bfloat16 [2048, 512], P('ch', 'tile'), may hold values from -0.125 to 0.125
Outputs:
- decoded: bfloat16 [2, 8, 32, 8, 30, 512], P(None, 'ch', 'tile')
The draws below stay inside these ranges and needn't reach their ends.
All inputs are finite; a program needn't handle non-finite values.
Results may differ from the reference program's by a relative error of at most 0.009.
Values may be sent and summed in bfloat16 or wider, within the bound.
No kernel may reach another device: no remote copies, remote signals or barrier semaphores. Data moves between devices by JAX's collectives and lax.ppermute only.
A program may use at most 192 MiB of HBM per device.

```python
import jax
import jax.numpy as jnp
from jax import lax

C = 512
HID = 2048
F = 8
GC = 4
B = 2
TR = 8
TC = 30
N_CH = 4
N_TILE = 32


def level_of(rng, shape, cuts, least, largest):
    level = 1.0
    for dim, blocks in cuts:
        heights = jax.random.uniform(jax.random.fold_in(jax.random.fold_in(rng, 6), dim), (blocks,), jnp.float32, least / len(cuts), largest / len(cuts))
        level = level * jnp.repeat(jnp.exp(heights), shape[dim] // blocks).reshape((-1,) + (1,) * (len(shape) - 1 - dim))
    return level


def centred(stream_key, dims, scale, limit, split=(), kind=jnp.bfloat16):
    values = jax.random.normal(stream_key, dims, jnp.float32) * scale
    if len(split) > 0:
        values = level_of(stream_key, dims, split, -0.22, 0.18) * values
    return jnp.clip(values, min=-limit, max=limit).astype(kind)


def setup_inputs(seed: int = 0) -> dict:
    streams_of = jax.random.split(jax.random.key(seed), 5)
    return {
        "latent": centred(streams_of[0], (B, F, N_TILE, TR, TC, C), 1.0, 6.0, ((2, 32), (5, 4))),
        "expand_weight": centred(streams_of[1], (C, 2, HID), C ** -0.5, 0.25, ((0, 32), (2, 4))),
        "depth_kernel": centred(streams_of[2], (3, 3, 3, 2, HID), 27 ** -0.5, 1.25, ((4, 4),), jnp.float32),
        "project_weight": centred(streams_of[3], (HID, C), HID ** -0.5, 0.125, ((0, 4), (1, 32))),
    }


def depthwise(padded_space, kernel):
    padded_all = jnp.pad(padded_space, ((0, 0), (1, 1), (0, 0), (0, 0), (0, 0), (0, 0)))
    frame_count = padded_all.shape[1] - 2
    row_count = padded_all.shape[2] - 2
    column_count = padded_all.shape[3] - 2
    accumulated = jnp.zeros(padded_all.shape[:1] + (frame_count, row_count, column_count) + padded_all.shape[4:], jnp.float32)
    for i in range(3):
        for j in range(3):
            for l in range(3):
                window = padded_all[:, i:i + frame_count, j:j + row_count, l:l + column_count]
                accumulated = accumulated + window.astype(jnp.float32) * kernel[i, j, l].astype(jnp.float32)
    return accumulated


def to_grid(tiled):
    clips, frames, tiles, rows, columns, chans = tiled.shape
    grouped = tiled.reshape(clips, frames, tiles // GC, GC, rows, columns, chans)
    return grouped.transpose(0, 1, 2, 4, 3, 5, 6).reshape(clips, frames, (tiles // GC) * rows, GC * columns, chans)


def to_tiles(grid):
    clips, frames, height, width, chans = grid.shape
    grouped = grid.reshape(clips, frames, height // TR, TR, GC, TC, chans)
    return grouped.transpose(0, 1, 2, 4, 3, 5, 6).reshape(clips, frames, (height // TR) * GC, TR, TC, chans)


def reference(latent, expand_weight, depth_kernel, project_weight):
    block_width = HID // N_CH
    grid = to_grid(latent)
    grid_wide = grid.astype(jnp.float32)
    summed = jnp.zeros(grid.shape, jnp.float32)
    for block_index in range(N_CH):
        offset = block_index * block_width
        weights = expand_weight[:, :, offset:offset + block_width].astype(jnp.float32)
        before = jnp.einsum("bfhwc,cgk->bfhwgk", grid_wide, weights)
        expanded = jax.nn.silu(before).astype(jnp.bfloat16)
        padded = jnp.pad(expanded, ((0, 0), (0, 0), (1, 1), (1, 1), (0, 0), (0, 0)))
        filtered = depthwise(padded, depth_kernel[..., offset:offset + block_width])
        hidden = (filtered[..., 0, :] * jax.nn.silu(filtered[..., 1, :])).astype(jnp.bfloat16)
        partial_value = jnp.dot(hidden, project_weight[offset:offset + block_width], preferred_element_type=jnp.float32)
        partial_value = lax.optimization_barrier(partial_value.astype(jnp.bfloat16)).astype(jnp.float32)
        summed = summed + partial_value
    return to_tiles((grid_wide + summed).astype(jnp.bfloat16))
```

```python
import functools

import jax
import jax.numpy as jnp
from jax import lax
from jax.experimental import pallas as pl
from jax.experimental.pallas import tpu as pltpu
from jax.sharding import PartitionSpec as P

F32 = jnp.float32
BF16 = jnp.bfloat16
BOTH = ("ch", "tile")


def device_pairs(move):
    pairs = []
    for ch in range(4):
        for tile in range(32):
            x, core = (ch // 2) * 2 + (tile // 4) % 2, ch % 2
            y, z = tile // 8, tile % 4
            to = move(x, y, z, core)
            if to is not None:
                tx, ty, tz, tc = to
                target = ((tx // 2) * 2 + tc) * 32 + (ty * 2 + tx % 2) * 4 + tz
                pairs.append((ch * 32 + tile, target))
    return pairs


def around(axis, by):
    def move(x, y, z, core):
        at = [x, y, z]
        at[axis] = (at[axis] + by) % 4
        return (*at, core)

    return device_pairs(move)


def column_step(by):
    def move(x, y, z, core):
        return (x, y, z + by, core) if 0 <= z + by < 4 else None

    return device_pairs(move)


def row_step(by):
    def move(x, y, z, core):
        row = y * 2 + x % 2 + by
        return ((x // 2) * 2 + row % 2, row // 2, z, core) if 0 <= row < 8 else None

    return device_pairs(move)


ACROSS = around(0, 2)
CORES = device_pairs(lambda x, y, z, core: (x, y, z, 1 - core))


def send(value, pairs):
    return lax.ppermute(value, BOTH, pairs)


def conv_taps(window, k_ref, gate, group):
    sums = [[None] * 3 for _ in range(4)]
    for j in range(3):
        taps = [[k_ref[(i * 3 + j) * 3 + l, gate, group] for l in range(3)] for i in range(3)]
        taps = [[jnp.concatenate([t, t], axis=0) for t in row] for row in taps]
        for slot in range(6):
            x = window(slot, j)
            for i in range(3):
                f = slot - i
                if 0 <= f < 4:
                    for l in range(3):
                        p = x * taps[i][l]
                        sums[f][l] = p if sums[f][l] is None else sums[f][l] + p
    out = []
    for f in range(4):
        left, centre, right = [s.astype(F32) for s in sums[f]]
        out.append(centre + pltpu.roll(left, 1, 0) + pltpu.roll(right, 31, 0))
    return out


ROWS = 1664
CHUNK = 416


def block_kernel(pos_ref, x0, x1, x2, x3, a0, a1, a2, a3, b0, b1, b2, b3, k_ref, out_ref,
                 x_scr, w_scr, e_scr, acc):
    xhi, core, y, z = pos_ref[0], pos_ref[1], pos_ref[2], pos_ref[3]
    base = 1 - xhi
    ch = xhi * 2 + core
    for r, ref in enumerate((x0, x1, x2, x3)):
        m = ch ^ r
        for b in range(2):
            x_scr[m, b, 0:1600, :] = ref[b]
            x_scr[m, b, 1600:ROWS, :] = jnp.zeros((ROWS - 1600, 128), BF16)
    for r, (a, b) in enumerate(((a0, b0), (a1, b1), (a2, b2), (a3, b3))):
        py, pz = (y + r) % 4, (z + r) % 4
        for o in range(4):
            for xlo in range(2):
                at_a = pl.ds(pl.multiple_of(((py * 2 + xlo) * 4 + o) * 16, 16), 16)
                at_b = pl.ds(pl.multiple_of(((o * 2 + xlo) * 4 + pz) * 16, 16), 16)
                for g in range(3):
                    w_scr[g, 0, at_a, :] = a[o, xlo, g]
                    w_scr[g, 1, at_b, :] = b[o, xlo, g]
    empty = jnp.where(base == 0, 5, 0)
    for buf in range(2):
        for g in range(4):
            e_scr[buf, g, pl.ds(pl.multiple_of(empty * 320, 64), 320), :] = jnp.zeros((320, 128), BF16)

    def expand(s, it, buf):
        b, c = s // 4, s % 4
        at = pl.ds(pl.multiple_of(it * CHUNK, 16), CHUNK)
        rows = jnp.concatenate([x_scr[m, b, at, :] for m in range(4)], axis=1)
        for g in range(2):
            w = w_scr[g, c // 2, :, pl.ds(pl.multiple_of((c % 2) * 256, 256), 256)]
            half = jnp.dot(rows, w, preferred_element_type=F32)
            e = (half * jnp.tanh(half) + half).astype(BF16)
            for q in range(2):
                to = pl.ds(pl.multiple_of(base * 320 + it * CHUNK, 16), CHUNK)
                e_scr[buf, g * 2 + q, to, :] = e[:, q * 128:(q + 1) * 128]

    def filter_rows(s, it, buf):
        b, c = s // 4, s % 4
        hidden, kept = [], []
        for r in range(2):
            h = it * 2 + r
            cols = []
            for q in range(2):
                parts = []
                for g in range(2):
                    def window(slot, j):
                        at = pl.multiple_of(slot * 320 + (h + j) * 32, 32)
                        return e_scr[buf, g * 2 + q, pl.ds(at, 32), :]

                    parts.append(conv_taps(window, k_ref, g, c * 2 + q))
                gated = []
                for f in range(4):
                    u = parts[1][f] * 0.5
                    gated.append((parts[0][f] * (u * jnp.tanh(u) + u)).astype(BF16))
                cols.append(jnp.concatenate(gated, axis=0))
            hidden.append(jnp.concatenate(cols, axis=1))
            for f in range(4):
                at = pl.ds(pl.multiple_of((f + xhi) * 320 + (h + 1) * 32, 32), 32)
                cells = jnp.concatenate([x_scr[m, b, at, :] for m in range(4)], axis=1)
                kept.append(jnp.where(core == f // 2, cells.astype(F32), 0.0))
        hidden = jnp.concatenate(hidden, axis=0)
        w = w_scr[2, c // 2, :, pl.ds(pl.multiple_of((c % 2) * 256, 256), 256)]
        y_new = lax.dot_general(hidden, w, (((1,), (1,)), ((), ())), preferred_element_type=F32)
        at = pl.ds(pl.multiple_of(it * 256, 256), 256)
        total = y_new + jnp.where(c == 0, jnp.concatenate(kept, axis=0), acc[at, :])
        acc[at, :] = total
        for r in range(2):
            for f in range(4):
                out_ref[f // 2 ^ core, b, f % 2, it * 2 + r] = total[(r * 4 + f) * 32:(r * 4 + f + 1) * 32]

    lax.fori_loop(0, 4, lambda it, _: (expand(0, it, 0), 0)[1], 0)

    def step(s, _):
        def inner(it, _):
            expand(jnp.minimum(s + 1, 7), it, 1 - s % 2)
            filter_rows(s, it, s % 2)
            return 0

        return lax.fori_loop(0, 4, inner, 0)

    lax.fori_loop(0, 8, step, 0)


def run_block(position, pieces, weights_a, weights_b, taps):
    vmem = pl.BlockSpec(memory_space=pltpu.VMEM)
    return pl.pallas_call(
        block_kernel,
        out_shape=jax.ShapeDtypeStruct((2, 2, 2, 8, 32, 512), F32),
        in_specs=[pl.BlockSpec(memory_space=pltpu.SMEM)] + [vmem] * 13,
        out_specs=vmem,
        scratch_shapes=[
            pltpu.VMEM((4, 2, ROWS, 128), BF16),
            pltpu.VMEM((3, 2, 512, 512), BF16),
            pltpu.VMEM((2, 4, 2048, 128), BF16),
            pltpu.VMEM((1024, 512), F32),
        ],
        compiler_params=pltpu.CompilerParams(vmem_limit_bytes=52 * 2**20),
        name="gated_block",
    )(position, *pieces, *weights_a, *weights_b, taps)


def gather_axis(piece, axis):
    return [piece] + [send(piece, around(axis, -by)) for by in (1, 2, 3)]


def in_order(pieces, own):
    return jnp.stack(pieces)[(jnp.arange(4) - own) % 4]


def on_device(latent, expand_weight, depth_kernel, project_weight):
    ch, tile = lax.axis_index("ch"), lax.axis_index("tile")
    xhi, core = ch // 2, ch % 2
    y, xlo, z = tile // 8, (tile // 4) % 2, tile % 4
    x = xhi * 2 + xlo

    cells = latent[:, :, 0]
    left = send(cells[:, :, :, -1:], column_step(1))
    right = send(cells[:, :, :, :1], column_step(-1))
    wide = jnp.concatenate([cells, right, left], axis=3)
    above = send(wide[:, :, -1:], row_step(1))
    below = send(wide[:, :, :1], row_step(-1))
    tall = jnp.concatenate([above, wide, below], axis=2)
    own = lax.dynamic_slice_in_dim(tall, 3 * xhi, 5, 1).reshape(2, 1600, 128)
    other = lax.dynamic_slice_in_dim(tall, 3 * (1 - xhi), 5, 1).reshape(2, 1600, 128)
    across = send(other, ACROSS)
    pieces = [own, send(own, CORES), across, send(across, CORES)]

    half = expand_weight * jnp.asarray(0.5, BF16)
    shard = jnp.stack([half[:, 0], half[:, 1], project_weight.T])
    by_x = in_order(gather_axis(shard, 0), x)
    half_a = in_order(gather_axis(by_x[:2], 2), z)
    half_b = in_order(gather_axis(by_x[2:], 1), y)
    weights_a = gather_axis(half_a, 1)
    weights_b = gather_axis(half_b, 2)

    taps = depth_kernel.reshape(27, 2, 4, 128)
    far = send(taps, ACROSS)
    taps = jnp.where(xhi == 0, jnp.concatenate([taps, far], axis=2), jnp.concatenate([far, taps], axis=2))
    taps = jnp.broadcast_to(taps.astype(BF16)[:, :, :, None], (27, 2, 8, 16, 128))

    position = jnp.stack([xhi, core, y, z]).astype(jnp.int32)
    partial = run_block(position, pieces, weights_a, weights_b, taps)
    received = send(partial[1].astype(BF16), CORES)
    total = (partial[0] + received.astype(F32)).astype(BF16)
    return total[:, :, None, :, :30]


def solution(mesh):
    return jax.shard_map(
        on_device,
        mesh=mesh,
        in_specs=(
            P(None, None, "tile", None, None, "ch"),
            P("tile", None, "ch"),
            P(None, None, None, None, "ch"),
            P("ch", "tile"),
        ),
        out_specs=P(None, "ch", "tile", None, None, None),
        check_vma=False,
    )
```

```python
import functools

import jax
import jax.numpy as jnp
from jax import lax
from jax.experimental import pallas as pl
from jax.experimental.pallas import tpu as pltpu
from jax.sharding import PartitionSpec as P

F32 = jnp.float32
BF16 = jnp.bfloat16
BOTH = ("ch", "tile")


def device_pairs(move):
    pairs = []
    for ch in range(4):
        for tile in range(32):
            x, core = (ch // 2) * 2 + (tile // 4) % 2, ch % 2
            y, z = tile // 8, tile % 4
            to = move(x, y, z, core)
            if to is not None:
                tx, ty, tz, tc = to
                target = ((tx // 2) * 2 + tc) * 32 + (ty * 2 + tx % 2) * 4 + tz
                pairs.append((ch * 32 + tile, target))
    return pairs


def around(axis, by):
    def move(x, y, z, core):
        at = [x, y, z]
        at[axis] = (at[axis] + by) % 4
        return (*at, core)

    return device_pairs(move)


def around_by_core(first, by):
    def move(x, y, z, core):
        at = [x, y, z]
        at[first if core == 0 else 3 - first] = (at[first if core == 0 else 3 - first] + by) % 4
        return (*at, core)

    return device_pairs(move)


def column_step(by):
    def move(x, y, z, core):
        return (x, y, z + by, core) if 0 <= z + by < 4 else None

    return device_pairs(move)


def row_step(by):
    def move(x, y, z, core):
        row = y * 2 + x % 2 + by
        return ((x // 2) * 2 + row % 2, row // 2, z, core) if 0 <= row < 8 else None

    return device_pairs(move)


ACROSS = around(0, 2)
BESIDE = device_pairs(lambda x, y, z, core: (x ^ 1, y, z, core))
DIAGONAL = device_pairs(lambda x, y, z, core: (x ^ 3, y, z, core))
CORES = device_pairs(lambda x, y, z, core: (x, y, z, 1 - core))


def send(value, pairs):
    return lax.ppermute(value, BOTH, pairs)


def forward(frames):
    d1, d2, d3, d4, d5 = frames
    a, b = d4 - 4.0 * d2, d3 - 4.0 * d1
    c, e = d4 - d2, d3 - d1
    e = e + e
    return a - d2, a + b, a - b, c + e, c - e, d5 - d3 - (e + e)


def backward(m):
    p, q, r, s = m[1] + m[2], m[1] - m[2], m[3] + m[4], m[3] - m[4]
    s = s + s
    return m[0] + p + r, q + s, p + 4.0 * r, q + 4.0 * s + m[5]


TAPS = (
    (1 / 4, 0, 0),
    (-1 / 6, -1 / 6, -1 / 6),
    (-1 / 6, 1 / 6, -1 / 6),
    (1 / 24, 1 / 12, 1 / 6),
    (1 / 24, -1 / 12, 1 / 6),
    (0, 0, 1),
)


def from_left(x):
    return jnp.concatenate([pltpu.roll(x[24:32], 1, 0), x[0:24]], axis=0)


def from_right(x):
    return jnp.concatenate([x[8:32], pltpu.roll(x[0:8], 7, 0)], axis=0)


def pack_kernel(pos_ref, c0, c1, c2, c3, x_ref, rows):
    xhi, core = pos_ref[0], pos_ref[1]
    ch = xhi * 2 + core

    def one(i, _):
        b, f = i // 5, i % 5
        to = jnp.where(xhi == 1, 4 - f, f)
        for r, cells in enumerate((c0, c1, c2, c3)):
            rows[r] = cells[pl.ds(pl.multiple_of(i * 320, 32), 320), :].astype(F32)
            for h in range(10):
                tile = jnp.concatenate([rows[r, pl.ds(h * 32 + q, 8, stride=4), :] for q in range(4)], axis=0)
                x_ref[ch ^ r, b, pl.ds(pl.multiple_of((h * 5 + to) * 32, 32), 32), :] = tile.astype(BF16)
        return 0

    lax.fori_loop(0, 10, one, 0)


def pack_cells(position, pieces):
    vmem = pl.BlockSpec(memory_space=pltpu.VMEM)
    return pl.pallas_call(
        pack_kernel,
        out_shape=jax.ShapeDtypeStruct((4, 2, 1600, 128), BF16),
        in_specs=[pl.BlockSpec(memory_space=pltpu.SMEM)] + [vmem] * 4,
        out_specs=vmem,
        scratch_shapes=[pltpu.VMEM((4, 320, 128), F32)],
        compiler_params=pltpu.CompilerParams(vmem_limit_bytes=32 * 2**20),
        name="pack_cells",
    )(position, *pieces)


def block_kernel(pos_ref, x_ref, p0, p1, p2, p3, k_ref, kept_ref, sent_ref, w_scr, t0, t1, acc, out_ref):
    xhi, core, y, z, xlo = (pos_ref[i] for i in range(5))
    for r, piece in enumerate((p0, p1, p2, p3)):
        for o in range(4):
            py = jnp.where(core == 0, y + r, y + o) % 4
            pz = jnp.where(core == 0, z + o, z + r) % 4
            for p in range(2):
                row = pl.multiple_of(((py * 2 + (xlo ^ p)) * 4 + pz) * 16, 16)
                for half in range(2):
                    for g in range(3):
                        w_scr[g, half, pl.ds(row, 16), :] = piece[o, half, p, g]

    def weights(g, c):
        return w_scr[g, c // 2, :, pl.ds(pl.multiple_of((c % 2) * 256, 256), 256)]

    def expand(s, row, g, t):
        b, c = s // 4, s % 4
        at = pl.ds(pl.multiple_of(row * 160, 32), 160)
        cells = jnp.concatenate([x_ref[m, b, at, :] for m in range(4)], axis=1)
        half = jnp.dot(cells, weights(g, c), preferred_element_type=F32)
        half = half * jnp.tanh(half) + half
        for q in range(2):
            frames = [half[f * 32:(f + 1) * 32, q * 128:(q + 1) * 128] for f in range(5)]
            for m, v in enumerate(forward(frames)):
                t[g * 2 + q, m, row] = v

    def filtered(t, group, g, tap, h):
        terms = []
        for m in range(6):
            sums = [None] * 3
            for j in range(3):
                x = t[group, m, h + j]
                for l in range(3):
                    p = x * k_ref[m, j * 3 + l, g, pl.ds(tap, 1), :]
                    sums[l] = p if sums[l] is None else sums[l] + p
            terms.append(sums[1] + from_left(sums[0]) + from_right(sums[2]))
        return backward(terms)

    def gated(t, c, h):
        cols = []
        for q in range(2):
            value = filtered(t, q, 0, c * 2 + q, h)
            gate = filtered(t, 2 + q, 1, c * 2 + q, h)
            cols.append(jnp.concatenate(
                [(v * (u * jnp.tanh(u) + u)).astype(BF16) for v, u in zip(value, gate)], axis=0))
        return jnp.concatenate(cols, axis=1)

    def project(s, it, hidden):
        b, c = s // 4, s % 4
        new = lax.dot_general(
            jnp.concatenate(hidden, axis=0), weights(2, c), (((1,), (1,)), ((), ())),
            preferred_element_type=F32)
        at = pl.ds(pl.multiple_of(it * 512, 512), 512)
        kept = []
        for r in range(4):
            for f in range(4):
                true = jnp.where(xhi == 1, 3 - f, f)
                cells_at = pl.ds(pl.multiple_of(((it * 4 + r + 1) * 5 + f) * 32, 32), 32)
                cells = jnp.concatenate([x_ref[m, b, cells_at, :] for m in range(4)], axis=1)
                kept.append(jnp.where(core == true // 2, cells.astype(F32), 0.0))
        total = new + jnp.where(c == 0, jnp.concatenate(kept, axis=0), acc[at, :])
        acc[at, :] = total
        for r in range(4):
            for f in range(4):
                true = jnp.where(xhi == 1, 3 - f, f)
                out_ref[true // 2 ^ core, b, true % 2, it * 4 + r] = total[(r * 4 + f) * 32:(r * 4 + f + 1) * 32]

    def first(row, _):
        for g in range(2):
            expand(0, row, g, t0)
        return 0

    lax.fori_loop(0, 10, first, 0)

    def step(s, now, later):
        def half(it, _):
            hidden = []
            for r in range(4):
                if later is not None:
                    for u in range(*((0, 3), (3, 6), (6, 8), (8, 10))[r]):
                        expand(s + 1, it * 5 + u % 5, u // 5, later)
                hidden.append(gated(now, s % 4, it * 4 + r))
            project(s, it, hidden)
            return 0

        lax.fori_loop(0, 2, half, 0)

    def pair(i, _):
        step(2 * i, t0, t1)
        step(2 * i + 1, t1, t0)
        return 0

    lax.fori_loop(0, 3, pair, 0)
    step(6, t0, t1)
    step(7, t1, None)

    def move(i, _):
        b, f, h = i // 16, i // 8 % 2, i % 8
        kept_ref[b, f, h] = out_ref[0, b, f, h]
        sent_ref[b, f, h] = out_ref[1, b, f, h].astype(BF16)
        return 0

    lax.fori_loop(0, 32, move, 0, unroll=2)


def run_block(position, cells, weights, taps):
    vmem = pl.BlockSpec(memory_space=pltpu.VMEM)
    return pl.pallas_call(
        block_kernel,
        out_shape=[jax.ShapeDtypeStruct((2, 2, 8, 32, 512), t) for t in (F32, BF16)],
        in_specs=[pl.BlockSpec(memory_space=pltpu.SMEM)] + [vmem] * 6,
        out_specs=[vmem] * 2,
        scratch_shapes=[
            pltpu.VMEM((3, 2, 512, 512), BF16),
            pltpu.VMEM((4, 6, 10, 32, 128), F32),
            pltpu.VMEM((4, 6, 10, 32, 128), F32),
            pltpu.VMEM((1024, 512), F32),
            pltpu.VMEM((2, 2, 2, 8, 32, 512), F32),
        ],
        compiler_params=pltpu.CompilerParams(vmem_limit_bytes=52 * 2**20),
        name="gated_block",
    )(position, cells, *weights, taps)


def finish_kernel(kept, received, out_ref, rows):
    def one(i, _):
        b, f, h = i // 16, i // 8 % 2, i % 8
        total = kept[b, f, h] + received[b, f, h].astype(F32)
        for v in range(4):
            for q in range(4):
                rows[v, pl.ds(q, 8, stride=4), :] = total[q * 8:(q + 1) * 8, v * 128:(v + 1) * 128]
        for v in range(4):
            out_ref[b, f, h, :, v * 128:(v + 1) * 128] = rows[v, 0:30, :].astype(BF16)
        return 0

    lax.fori_loop(0, 32, one, 0)


def finish(kept, received):
    vmem = pl.BlockSpec(memory_space=pltpu.VMEM)
    return pl.pallas_call(
        finish_kernel,
        out_shape=jax.ShapeDtypeStruct((2, 2, 8, 30, 512), BF16),
        in_specs=[vmem] * 2,
        out_specs=vmem,
        scratch_shapes=[pltpu.VMEM((4, 32, 128), F32)],
        compiler_params=pltpu.CompilerParams(vmem_limit_bytes=32 * 2**20),
        name="finish",
    )(kept, received)


def on_device(latent, expand_weight, depth_kernel, project_weight):
    ch, tile = lax.axis_index("ch"), lax.axis_index("tile")
    xhi, core = ch // 2, ch % 2
    y, xlo, z = tile // 8, (tile // 4) % 2, tile % 4
    position = jnp.stack([xhi, core, y, z, xlo]).astype(jnp.int32)
    cells = latent[:, :, 0]

    half = expand_weight * jnp.asarray(0.5, BF16)
    shard = jnp.stack([half[:, 0], half[:, 1], project_weight.T])
    shard = jnp.stack([shard, send(shard, BESIDE), send(shard, ACROSS), send(shard, DIAGONAL)])
    shard = shard.reshape(2, 2, 3, 16, 512)
    above = send(cells[:, :, 7], row_step(1))
    below = send(cells[:, :, 0], row_step(-1))

    def edge(column):
        return jnp.concatenate([above[:, :, None, column], cells[:, :, :, column], below[:, :, None, column]], axis=2)

    first, last, shard = lax.optimization_barrier((edge(0), edge(29), shard))
    shard = jnp.stack([shard] + [send(shard, around_by_core(2, -by)) for by in (1, 2, 3)])
    left = send(last, column_step(1))
    right = send(first, column_step(-1))
    tall = jnp.concatenate([above[:, :, None], cells, below[:, :, None]], axis=2)
    tall = jnp.concatenate([tall, right[:, :, :, None], left[:, :, :, None]], axis=3)
    own = lax.dynamic_slice_in_dim(tall, 3 * xhi, 5, 1).reshape(3200, 128)
    other = lax.dynamic_slice_in_dim(tall, 3 * (1 - xhi), 5, 1).reshape(3200, 128)
    taps = depth_kernel.reshape(3, 9, 2, 4, 128)
    taps = jnp.where(xhi == 1, taps[::-1], taps)
    other, shard = lax.optimization_barrier((jnp.concatenate([other, taps.reshape(216, 128).astype(BF16)]), shard))
    across = send(other, ACROSS)
    weights = [shard] + [send(shard, around_by_core(1, -by)) for by in (1, 2, 3)]
    across, weights[1] = lax.optimization_barrier((across, weights[1]))
    there = [send(own, CORES), send(across[:3200], CORES)]
    taps = jnp.concatenate([taps, across[3200:].astype(F32).reshape(3, 9, 2, 4, 128)[::-1]], axis=3)
    scale = jnp.array([1.0, 0.5], F32)[None, :, None, None]
    taps = jnp.stack([sum(row[i] * taps[i] for i in range(3) if row[i]) * scale for row in TAPS])

    packed = pack_cells(position, [own, there[0], across, there[1]])
    kept, sent = run_block(position, packed, weights, taps)
    return finish(kept, send(sent, CORES))[:, :, None]


def solution(mesh):
    return jax.shard_map(
        on_device,
        mesh=mesh,
        in_specs=(
            P(None, None, "tile", None, None, "ch"),
            P("tile", None, "ch"),
            P(None, None, None, None, "ch"),
            P("ch", "tile"),
        ),
        out_specs=P(None, "ch", "tile", None, None, None),
        check_vma=False,
    )
```

```python
import functools

import jax
import jax.numpy as jnp
from jax import lax
from jax.experimental import pallas as pl
from jax.experimental.pallas import tpu as pltpu
from jax.sharding import PartitionSpec as P

F32 = jnp.float32
BF16 = jnp.bfloat16
BOTH = ("ch", "tile")


def device_pairs(move):
    pairs = []
    for ch in range(4):
        for tile in range(32):
            x, core = (ch // 2) * 2 + (tile // 4) % 2, ch % 2
            y, z = tile // 8, tile % 4
            to = move(x, y, z, core)
            if to is not None:
                tx, ty, tz, tc = to
                target = ((tx // 2) * 2 + tc) * 32 + (ty * 2 + tx % 2) * 4 + tz
                pairs.append((ch * 32 + tile, target))
    return pairs


def around(axis, by):
    def move(x, y, z, core):
        at = [x, y, z]
        at[axis] = (at[axis] + by) % 4
        return (*at, core)

    return device_pairs(move)


def around_by_core(first, by):
    def move(x, y, z, core):
        at = [x, y, z]
        at[first if core == 0 else 3 - first] = (at[first if core == 0 else 3 - first] + by) % 4
        return (*at, core)

    return device_pairs(move)


def column_step(by):
    def move(x, y, z, core):
        return (x, y, z + by, core) if 0 <= z + by < 4 else None

    return device_pairs(move)


def row_step(by):
    def move(x, y, z, core):
        row = y * 2 + x % 2 + by
        return ((x // 2) * 2 + row % 2, row // 2, z, core) if 0 <= row < 8 else None

    return device_pairs(move)


ACROSS = around(0, 2)
BESIDE = device_pairs(lambda x, y, z, core: (x ^ 1, y, z, core))
DIAGONAL = device_pairs(lambda x, y, z, core: (x ^ 3, y, z, core))
CORES = device_pairs(lambda x, y, z, core: (x, y, z, 1 - core))


def send(value, pairs):
    return lax.ppermute(value, BOTH, pairs)


def forward(frames):
    d1, d2, d3, d4, d5 = frames
    a, b = d4 - 4.0 * d2, d3 - 4.0 * d1
    c, e = d4 - d2, d3 - d1
    e = e + e
    return a - d2, a + b, a - b, c + e, c - e, d5 - d3 - (e + e)


def backward(m):
    p, q, r, s = m[1] + m[2], m[1] - m[2], m[3] + m[4], m[3] - m[4]
    s = s + s
    return m[0] + p + r, q + s, p + 4.0 * r, q + 4.0 * s + m[5]


TAPS = (
    (1 / 4, 0, 0),
    (-1 / 6, -1 / 6, -1 / 6),
    (-1 / 6, 1 / 6, -1 / 6),
    (1 / 24, 1 / 12, 1 / 6),
    (1 / 24, -1 / 12, 1 / 6),
    (0, 0, 1),
)


ROW_TAPS = ((1, 0, 0), (1 / 2, 1 / 2, 1 / 2), (1 / 2, -1 / 2, 1 / 2), (0, 0, 1))


def from_left(x):
    return jnp.concatenate([pltpu.roll(x[24:32], 1, 0), x[0:24]], axis=0)


def from_right(x):
    return jnp.concatenate([x[8:32], pltpu.roll(x[0:8], 7, 0)], axis=0)


def pack_kernel(pos_ref, m0, m1, m2, m3, own_rim, across_rim, core_rim, x_ref, rows):
    xhi, core = pos_ref[0], pos_ref[1]
    ch = xhi * 2 + core

    def one(i, _):
        b, f = i // 5, i % 5
        to = jnp.where(xhi == 1, 4 - f, f)
        for r, main in enumerate((m0, m1, m2, m3)):
            rim = (own_rim, core_rim, across_rim, core_rim)[r]
            at = pl.multiple_of(i * 80 + (800 if r == 3 else 0), 16)
            strips = rim[pl.ds(at, 80), :].astype(F32)
            rows[r, 0:32, :] = strips[0:32]
            rows[r, 288:320, :] = strips[32:64]
            for h in range(8):
                rows[r, (h + 1) * 32:(h + 1) * 32 + 32, :] = main[pl.ds(pl.multiple_of(i * 256 + h * 32, 32), 32), :].astype(F32)
            rows[r, pl.ds(62, 8, stride=32), :] = strips[64:72]
            rows[r, pl.ds(63, 8, stride=32), :] = strips[72:80]
            for h in range(10):
                tile = jnp.concatenate([rows[r, pl.ds(h * 32 + q, 8, stride=4), :] for q in range(4)], axis=0)
                x_ref[ch ^ r, b, pl.ds(pl.multiple_of((h * 5 + to) * 32, 32), 32), :] = tile.astype(BF16)
        return 0

    lax.fori_loop(0, 10, one, 0)


def pack_cells(position, pieces):
    vmem = pl.BlockSpec(memory_space=pltpu.VMEM)
    return pl.pallas_call(
        pack_kernel,
        out_shape=jax.ShapeDtypeStruct((4, 2, 1600, 128), BF16),
        in_specs=[pl.BlockSpec(memory_space=pltpu.SMEM)] + [vmem] * 7,
        out_specs=vmem,
        scratch_shapes=[pltpu.VMEM((4, 320, 128), F32)],
        compiler_params=pltpu.CompilerParams(vmem_limit_bytes=32 * 2**20),
        name="pack_cells",
    )(position, *pieces)


def block_kernel(pos_ref, x_ref, p0, p1, p2, p3, k_ref, kept_ref, sent_ref, w_scr, wp_scr, t0, t1, hidden, acc, rows):
    xhi, core, y, z, xlo = (pos_ref[i] for i in range(5))
    for r, piece in enumerate((p0, p1, p2, p3)):
        for o in range(4):
            py = jnp.where(core == 0, y + r, y + o) % 4
            pz = jnp.where(core == 0, z + o, z + r) % 4
            for p in range(2):
                row = pl.ds(pl.multiple_of(((py * 2 + (xlo ^ p)) * 4 + pz) * 16, 16), 16)
                for half in range(2):
                    for g in range(2):
                        w_scr[g, half, row, :] = piece[o, half, p, g]
                    wp_scr[row, half * 512:(half + 1) * 512] = piece[o, half, p, 2]

    def weights(g, c):
        return w_scr[g, c // 2, :, pl.ds(pl.multiple_of((c % 2) * 256, 256), 256)]

    def expand(s, row, g, t):
        b, c = s // 4, s % 4
        at = pl.ds(pl.multiple_of(row * 160, 32), 160)
        cells = jnp.concatenate([x_ref[m, b, at, :] for m in range(4)], axis=1)
        half = jnp.dot(cells, weights(g, c), preferred_element_type=F32)
        half = half * jnp.tanh(half) + half
        for q in range(2):
            frames = [half[f * 32:(f + 1) * 32, q * 128:(q + 1) * 128] for f in range(5)]
            for m, v in enumerate(forward(frames)):
                t[g * 2 + q, m, row] = v

    def filtered(t, group, g, tap, h):
        terms = [[], []]
        for m in range(6):
            d = [t[group, m, h + i] for i in range(4)]
            d = [d[0] - d[2], d[1] + d[2], d[2] - d[1], d[1] - d[3]]
            p = []
            for i in range(4):
                x = [d[i] * k_ref[m, i * 3 + l, g, pl.ds(tap, 1), :] for l in range(3)]
                p.append(x[1] + from_left(x[0]) + from_right(x[2]))
            terms[0].append(p[0] + p[1] + p[2])
            terms[1].append(p[1] - p[2] - p[3])
        return [backward(m) for m in terms]

    def gate_rows(t, c, h):
        for q in range(2):
            value = filtered(t, q, 0, c * 2 + q, h)
            gate = filtered(t, 2 + q, 1, c * 2 + q, h)
            for r in range(2):
                both = [(v * (u * jnp.tanh(u) + u)).astype(BF16) for v, u in zip(value[r], gate[r])]
                at = pl.ds(pl.multiple_of((h + r) * 128, 128), 128)
                hidden[c, at, q * 128:(q + 1) * 128] = jnp.concatenate(both, axis=0)

    def project(b):
        def part(i, _):
            at = pl.ds(pl.multiple_of(i * 512, 512), 512)
            units = jnp.concatenate([hidden[c, at, :] for c in range(4)], axis=1)
            new = lax.dot_general(units, wp_scr[...], (((1,), (1,)), ((), ())), preferred_element_type=F32)
            acc[b, at, :] = new
            return 0

        lax.fori_loop(0, 2, part, 0)

    def first(row, _):
        for g in range(2):
            expand(0, row, g, t0)
        return 0

    lax.fori_loop(0, 10, first, 0)

    def step(s, now, later):
        def half(it, _):
            for r in range(2):
                gate_rows(now, s % 4, it * 4 + 2 * r)
                if later is not None:
                    for u in range(5):
                        expand(s + 1, it * 5 + u, r, later)
            return 0

        lax.fori_loop(0, 2, half, 0)

    def pair(i, _):
        step(2 * i, t0, t1)
        step(2 * i + 1, t1, t0)

        @pl.when(i == 1)
        def _():
            project(0)

        return 0

    lax.fori_loop(0, 3, pair, 0)
    step(6, t0, t1)
    step(7, t1, None)
    project(1)

    def move(i, _):
        b, f, h = i // 16, i // 8 % 2, i % 8
        for slot in range(2):
            true = (core ^ slot) * 2 + f
            frame = jnp.where(xhi == 1, 3 - true, true)
            at = pl.ds(pl.multiple_of((h * 4 + frame) * 32, 32), 32)
            total = acc[b, at, :]
            if slot == 0:
                cells_at = pl.ds(pl.multiple_of(((h + 1) * 5 + frame) * 32, 32), 32)
                cells = jnp.concatenate([x_ref[m, b, cells_at, :] for m in range(4)], axis=1)
                total = total + cells.astype(F32)
            for v in range(4):
                for q in range(4):
                    rows[slot * 4 + v, pl.ds(q, 8, stride=4), :] = total[q * 8:(q + 1) * 8, v * 128:(v + 1) * 128]
            total = jnp.concatenate([rows[slot * 4 + v] for v in range(4)], axis=1)
            if slot == 0:
                kept_ref[b, f, h] = total
            else:
                sent_ref[b, f, h] = total.astype(BF16)
        return 0

    lax.fori_loop(0, 32, move, 0)


def run_block(position, cells, weights, taps):
    vmem = pl.BlockSpec(memory_space=pltpu.VMEM)
    return pl.pallas_call(
        block_kernel,
        out_shape=[jax.ShapeDtypeStruct((2, 2, 8, 32, 512), t) for t in (F32, BF16)],
        in_specs=[pl.BlockSpec(memory_space=pltpu.SMEM)] + [vmem] * 6,
        out_specs=[vmem] * 2,
        scratch_shapes=[
            pltpu.VMEM((2, 2, 512, 512), BF16),
            pltpu.VMEM((512, 1024), BF16),
            pltpu.VMEM((4, 6, 10, 32, 128), F32),
            pltpu.VMEM((4, 6, 10, 32, 128), F32),
            pltpu.VMEM((4, 1024, 256), BF16),
            pltpu.VMEM((2, 1024, 512), F32),
            pltpu.VMEM((8, 32, 128), F32),
        ],
        compiler_params=pltpu.CompilerParams(vmem_limit_bytes=52 * 2**20),
        name="gated_block",
    )(position, cells, *weights, taps)


def on_device(latent, expand_weight, depth_kernel, project_weight):
    ch, tile = lax.axis_index("ch"), lax.axis_index("tile")
    xhi, core = ch // 2, ch % 2
    y, xlo, z = tile // 8, (tile // 4) % 2, tile % 4
    position = jnp.stack([xhi, core, y, z, xlo]).astype(jnp.int32)
    cells = latent[:, :, 0]

    half = expand_weight * jnp.asarray(0.5, BF16)
    shard = jnp.stack([half[:, 0], half[:, 1], project_weight.T])
    shard = jnp.stack([shard, send(shard, BESIDE), send(shard, ACROSS), send(shard, DIAGONAL)])
    shard = shard.reshape(2, 2, 3, 16, 512)
    above = send(cells[:, :, 7], row_step(1))
    below = send(cells[:, :, 0], row_step(-1))

    shard, cells = lax.optimization_barrier((shard, cells))
    near = [shard] + [send(shard, around_by_core(2, -by)) for by in (1, 2, 3)]
    wide = jnp.pad(cells, ((0, 0),) * 3 + ((0, 2), (0, 0)))
    own = lax.dynamic_slice_in_dim(wide, 3 * xhi, 5, 1).reshape(2560, 128)
    across = send(lax.dynamic_slice_in_dim(wide, 3 * (1 - xhi), 5, 1).reshape(2560, 128), ACROSS)
    own_there = send(own, CORES)

    def edge(column):
        return jnp.concatenate([above[:, :, None, column], cells[:, :, :, column], below[:, :, None, column]], axis=2)

    shard, first, last = lax.optimization_barrier((jnp.stack(near), edge(0), edge(29)))
    weights = [shard] + [send(shard, around_by_core(1, -by)) for by in (1, 2, 3)]
    left = send(last, column_step(1))
    right = send(first, column_step(-1))

    def rim(start):
        a, b, l, r = (lax.dynamic_slice_in_dim(v, start, 5, 1) for v in (above, below, left, right))
        return jnp.concatenate(
            [a, r[:, :, :1], l[:, :, :1], b, r[:, :, 9:], l[:, :, 9:], r[:, :, 1:9], l[:, :, 1:9]],
            axis=2).reshape(800, 128)

    taps = depth_kernel.reshape(3, 9, 2, 4, 128)
    taps = jnp.where(xhi == 1, taps[::-1], taps)
    own_rim = rim(3 * xhi)
    across_rim = send(jnp.concatenate([rim(3 * (1 - xhi)), taps.reshape(216, 128).astype(BF16)]), ACROSS)
    across, across_rim, weights[1] = lax.optimization_barrier((across, across_rim, weights[1]))
    core_rim = send(jnp.concatenate([own_rim, across_rim[:800]]), CORES)
    pieces = [own, own_there, across, send(across, CORES), own_rim, across_rim, core_rim]
    taps = jnp.concatenate([taps, across_rim[800:].astype(F32).reshape(3, 9, 2, 4, 128)[::-1]], axis=3)
    by_frame = [sum(row[i] * taps[i] for i in range(3) if row[i]) for row in TAPS]
    by_frame = jnp.stack(by_frame).reshape(6, 3, 3, 2, 8, 128)
    by_row = [sum(row[j] * by_frame[:, j] for j in range(3) if row[j]) for row in ROW_TAPS]
    taps = jnp.stack(by_row, axis=1).reshape(6, 12, 2, 8, 128)
    taps = taps * jnp.array([1.0, 0.5], F32)[None, None, :, None, None]

    packed = pack_cells(position, pieces)
    kept, sent = run_block(position, packed, weights, taps)
    total = kept + send(sent, CORES).astype(F32)
    return total[:, :, None, :, :30].astype(BF16)


def solution(mesh):
    return jax.shard_map(
        on_device,
        mesh=mesh,
        in_specs=(
            P(None, None, "tile", None, None, "ch"),
            P("tile", None, "ch"),
            P(None, None, None, None, "ch"),
            P("ch", "tile"),
        ),
        out_specs=P(None, "ch", "tile", None, None, None),
        check_vma=False,
    )
```

```python
import functools

import jax
import jax.numpy as jnp
from jax import lax
from jax.experimental import pallas as pl
from jax.experimental.pallas import tpu as pltpu
from jax.sharding import PartitionSpec as P

F32 = jnp.float32
BF16 = jnp.bfloat16
BOTH = ("ch", "tile")


def device_pairs(move):
    pairs = []
    for ch in range(4):
        for tile in range(32):
            x, core = (ch // 2) * 2 + (tile // 4) % 2, ch % 2
            y, z = tile // 8, tile % 4
            to = move(x, y, z, core)
            if to is not None:
                tx, ty, tz, tc = to
                target = ((tx // 2) * 2 + tc) * 32 + (ty * 2 + tx % 2) * 4 + tz
                pairs.append((ch * 32 + tile, target))
    return pairs


def around(axis, by):
    def move(x, y, z, core):
        at = [x, y, z]
        at[axis] = (at[axis] + by) % 4
        return (*at, core)

    return device_pairs(move)


def around_by_core(first, by):
    def move(x, y, z, core):
        at = [x, y, z]
        at[first if core == 0 else 3 - first] = (at[first if core == 0 else 3 - first] + by) % 4
        return (*at, core)

    return device_pairs(move)


def column_step(by):
    def move(x, y, z, core):
        return (x, y, z + by, core) if 0 <= z + by < 4 else None

    return device_pairs(move)


def row_step(by):
    def move(x, y, z, core):
        row = y * 2 + x % 2 + by
        return ((x // 2) * 2 + row % 2, row // 2, z, core) if 0 <= row < 8 else None

    return device_pairs(move)


ACROSS = around(0, 2)
BESIDE = device_pairs(lambda x, y, z, core: (x ^ 1, y, z, core))
DIAGONAL = device_pairs(lambda x, y, z, core: (x ^ 3, y, z, core))
CORES = device_pairs(lambda x, y, z, core: (x, y, z, 1 - core))


def send(value, pairs):
    return lax.ppermute(value, BOTH, pairs)


def forward(frames):
    d1, d2, d3, d4, d5 = frames
    a, b = d4 - 4.0 * d2, d3 - 4.0 * d1
    c, e = d4 - d2, d3 - d1
    e = e + e
    return a - d2, a + b, a - b, c + e, c - e, d5 - d3 - (e + e)


def backward(m):
    p, q, r, s = m[1] + m[2], m[1] - m[2], m[3] + m[4], m[3] - m[4]
    s = s + s
    return m[0] + p + r, q + s, p + 4.0 * r, q + 4.0 * s + m[5]


TAPS = (
    (1 / 4, 0, 0),
    (-1 / 6, -1 / 6, -1 / 6),
    (-1 / 6, 1 / 6, -1 / 6),
    (1 / 24, 1 / 12, 1 / 6),
    (1 / 24, -1 / 12, 1 / 6),
    (0, 0, 1),
)


ROW_TAPS = ((1, 0, 0), (1 / 2, 1 / 2, 1 / 2), (1 / 2, -1 / 2, 1 / 2), (0, 0, 1))


def from_left(x):
    return jnp.concatenate([pltpu.roll(x[24:32], 1, 0), x[0:24]], axis=0)


def from_right(x):
    return jnp.concatenate([x[8:32], pltpu.roll(x[0:8], 7, 0)], axis=0)


def rim_kernel(pos_ref, above, below, left, right, own_ref, other_ref, tile, edge):
    xhi = pos_ref[0]

    def one(i, _):
        for out, start in ((own_ref, 3 * xhi), (other_ref, 3 * (1 - xhi))):
            b, f = i // 5, start + i % 5
            tile[0:30, :] = above[b, f].astype(F32)
            tile[32:62, :] = below[b, f].astype(F32)
            for k, side in enumerate((right, left)):
                edge[k, 0:10, :] = side[b, f].astype(F32)
                tile[30 + k:31 + k, :] = edge[k, 0:1, :]
                tile[62 + k:63 + k, :] = edge[k, 9:10, :]
                tile[64 + 8 * k:72 + 8 * k, :] = edge[k, 1:9, :]
            out[pl.ds(pl.multiple_of(i * 80, 16), 80), :] = tile[...].astype(BF16)
        return 0

    lax.fori_loop(0, 10, one, 0)


def pack_rims(position, above, below, left, right):
    vmem = pl.BlockSpec(memory_space=pltpu.VMEM)
    return pl.pallas_call(
        rim_kernel,
        out_shape=[jax.ShapeDtypeStruct((800, 128), BF16)] * 2,
        in_specs=[pl.BlockSpec(memory_space=pltpu.SMEM)] + [vmem] * 4,
        out_specs=[vmem] * 2,
        scratch_shapes=[pltpu.VMEM((80, 128), F32), pltpu.VMEM((2, 16, 128), F32)],
        compiler_params=pltpu.CompilerParams(vmem_limit_bytes=16 * 2**20),
        name="pack_rims",
    )(position, above, below, left, right)


def pack_kernel(pos_ref, m0, m1, m2, m3, r0, r1, r2, r3, x_ref, rows):
    xhi = pos_ref[0]
    ch = xhi * 2 + pos_ref[1]
    mains, rims = (m0, m1, m2, m3), (r0, r1, r2, r3)

    def one(i, _):
        b, f = i // 5, i % 5
        to = jnp.where(xhi == 1, 4 - f, f)
        for r, (main, rim) in enumerate(zip(mains, rims)):
            strips = rim[pl.ds(pl.multiple_of(i * 80, 16), 80), :].astype(F32)
            rows[r, 0:32, :] = strips[0:32]
            rows[r, 288:320, :] = strips[32:64]
            for h in range(8):
                at = pl.ds(pl.multiple_of(i * 256 + h * 32, 32), 32)
                rows[r, (h + 1) * 32:(h + 2) * 32, :] = main[at, :].astype(F32)
            rows[r, pl.ds(62, 8, stride=32), :] = strips[64:72]
            rows[r, pl.ds(63, 8, stride=32), :] = strips[72:80]
            for h in range(10):
                tile = jnp.concatenate([rows[r, pl.ds(h * 32 + q, 8, stride=4), :] for q in range(4)], axis=0)
                x_ref[ch ^ r, b, pl.ds(pl.multiple_of((h * 5 + to) * 32, 32), 32), :] = tile.astype(BF16)
        return 0

    lax.fori_loop(0, 10, one, 0)


def pack_cells(position, mains, rims):
    vmem = pl.BlockSpec(memory_space=pltpu.VMEM)
    return pl.pallas_call(
        pack_kernel,
        out_shape=jax.ShapeDtypeStruct((4, 2, 1600, 128), BF16),
        in_specs=[pl.BlockSpec(memory_space=pltpu.SMEM)] + [vmem] * 8,
        out_specs=vmem,
        scratch_shapes=[pltpu.VMEM((4, 320, 128), F32)],
        compiler_params=pltpu.CompilerParams(vmem_limit_bytes=16 * 2**20),
        name="pack_cells",
    )(position, *mains, *rims)


def block_kernel(pos_ref, x_ref, p0, p1, p2, p3, k_ref, kept_ref, sent_ref,
                 w_scr, wp_scr, t0, t1, hidden, acc, rows):
    xhi, core, y, z, xlo = (pos_ref[i] for i in range(5))
    for r, piece in enumerate((p0, p1, p2, p3)):
        for o in range(4):
            py = jnp.where(core == 0, y + r, y + o) % 4
            pz = jnp.where(core == 0, z + o, z + r) % 4
            for p in range(2):
                row = pl.ds(pl.multiple_of(((py * 2 + (xlo ^ p)) * 4 + pz) * 16, 16), 16)
                for half in range(2):
                    for g in range(2):
                        w_scr[g, half, row, :] = piece[o, half, p, g]
                    wp_scr[row, half * 512:(half + 1) * 512] = piece[o, half, p, 2]

    def weights(g, c):
        return w_scr[g, c // 2, :, pl.ds(pl.multiple_of((c % 2) * 256, 256), 256)]

    def expand(s, row, g, t):
        b, c = s // 4, s % 4
        at = pl.ds(pl.multiple_of(row * 160, 32), 160)
        cells = jnp.concatenate([x_ref[m, b, at, :] for m in range(4)], axis=1)
        half = jnp.dot(cells, weights(g, c), preferred_element_type=F32)
        half = half * jnp.tanh(half) + half
        for q in range(2):
            frames = [half[f * 32:(f + 1) * 32, q * 128:(q + 1) * 128] for f in range(5)]
            for m, v in enumerate(forward(frames)):
                t[g * 2 + q, m, row] = v

    def filtered(t, group, g, tap, h):
        terms = [[], []]
        for m in range(6):
            d = [t[group, m, h + i] for i in range(4)]
            d = [d[0] - d[2], d[1] + d[2], d[2] - d[1], d[1] - d[3]]
            p = []
            for i in range(4):
                x = [d[i] * k_ref[m, i * 3 + l, g, pl.ds(tap, 1), :] for l in range(3)]
                p.append(x[1] + from_left(x[0]) + from_right(x[2]))
            terms[0].append(p[0] + p[1] + p[2])
            terms[1].append(p[1] - p[2] - p[3])
        return [backward(m) for m in terms]

    def gate_rows(t, c, h):
        for q in range(2):
            value = filtered(t, q, 0, c * 2 + q, h)
            gate = filtered(t, 2 + q, 1, c * 2 + q, h)
            for r in range(2):
                both = [(v * (u * jnp.tanh(u) + u)).astype(BF16) for v, u in zip(value[r], gate[r])]
                at = pl.ds(pl.multiple_of((h + r) * 128, 128), 128)
                hidden[c, at, q * 128:(q + 1) * 128] = jnp.concatenate(both, axis=0)

    def project(b):
        def part(i, _):
            at = pl.ds(pl.multiple_of(i * 512, 512), 512)
            units = jnp.concatenate([hidden[c, at, :] for c in range(4)], axis=1)
            new = lax.dot_general(units, wp_scr[...], (((1,), (1,)), ((), ())), preferred_element_type=F32)
            acc[b, at, :] = new
            return 0

        lax.fori_loop(0, 2, part, 0)

    def first(row, _):
        for g in range(2):
            expand(0, row, g, t0)
        return 0

    lax.fori_loop(0, 10, first, 0)

    def step(s, now, later):
        def half(it, _):
            for r in range(2):
                gate_rows(now, s % 4, it * 4 + 2 * r)
                if later is not None:
                    for u in range(5):
                        expand(s + 1, it * 5 + u, r, later)
            return 0

        lax.fori_loop(0, 2, half, 0)

    def pair(i, _):
        step(2 * i, t0, t1)
        step(2 * i + 1, t1, t0)

        @pl.when(i == 1)
        def _():
            project(0)

        return 0

    lax.fori_loop(0, 3, pair, 0)
    step(6, t0, t1)
    step(7, t1, None)
    project(1)

    def move(i, _):
        b, f, h = i // 16, i // 8 % 2, i % 8
        for slot in range(2):
            true = (core ^ slot) * 2 + f
            frame = jnp.where(xhi == 1, 3 - true, true)
            at = pl.ds(pl.multiple_of((h * 4 + frame) * 32, 32), 32)
            total = acc[b, at, :]
            if slot == 0:
                cells_at = pl.ds(pl.multiple_of(((h + 1) * 5 + frame) * 32, 32), 32)
                cells = jnp.concatenate([x_ref[m, b, cells_at, :] for m in range(4)], axis=1)
                total = total + cells.astype(F32)
            for v in range(4):
                for q in range(4):
                    rows[slot * 4 + v, pl.ds(q, 8, stride=4), :] = total[q * 8:(q + 1) * 8, v * 128:(v + 1) * 128]
            total = jnp.concatenate([rows[slot * 4 + v] for v in range(4)], axis=1)
            if slot == 0:
                kept_ref[b, f, h] = total
            else:
                sent_ref[b, f, h] = total.astype(BF16)
        return 0

    lax.fori_loop(0, 32, move, 0)


def run_block(position, cells, weights, taps):
    vmem = pl.BlockSpec(memory_space=pltpu.VMEM)
    return pl.pallas_call(
        block_kernel,
        out_shape=[jax.ShapeDtypeStruct((2, 2, 8, 32, 512), t) for t in (F32, BF16)],
        in_specs=[pl.BlockSpec(memory_space=pltpu.SMEM)] + [vmem] * 6,
        out_specs=[vmem] * 2,
        scratch_shapes=[
            pltpu.VMEM((2, 2, 512, 512), BF16),
            pltpu.VMEM((512, 1024), BF16),
            pltpu.VMEM((4, 6, 10, 32, 128), F32),
            pltpu.VMEM((4, 6, 10, 32, 128), F32),
            pltpu.VMEM((4, 1024, 256), BF16),
            pltpu.VMEM((2, 1024, 512), F32),
            pltpu.VMEM((8, 32, 128), F32),
        ],
        compiler_params=pltpu.CompilerParams(vmem_limit_bytes=52 * 2**20),
        name="gated_block",
    )(position, cells, *weights, taps)


def on_device(latent, expand_weight, depth_kernel, project_weight):
    ch, tile = lax.axis_index("ch"), lax.axis_index("tile")
    xhi, core = ch // 2, ch % 2
    y, xlo, z = tile // 8, (tile // 4) % 2, tile % 4
    position = jnp.stack([xhi, core, y, z, xlo]).astype(jnp.int32)
    cells = latent[:, :, 0]

    half = expand_weight * jnp.asarray(0.5, BF16)
    shard = jnp.stack([half[:, 0], half[:, 1], project_weight.T])
    taps = depth_kernel.reshape(3, 9, 2, 512)
    back = taps[::-1]
    there = jnp.where(xhi == 1, taps, back).astype(BF16).reshape(54, 512)
    taps = jnp.where(xhi == 1, back, taps)
    far = send(jnp.concatenate([shard.reshape(48, 512), there]), ACROSS)
    shard = jnp.stack([shard, send(shard, BESIDE), far[:48].reshape(3, 16, 512), send(shard, DIAGONAL)])
    shard = shard.reshape(2, 2, 3, 16, 512)
    taps = jnp.concatenate(
        [taps.reshape(3, 9, 2, 4, 128), far[48:].astype(F32).reshape(3, 9, 2, 4, 128)], axis=3)
    above = send(cells[:, :, 7], row_step(1))
    below = send(cells[:, :, 0], row_step(-1))

    shard, cells = lax.optimization_barrier((shard, cells))
    near = [shard] + [send(shard, around_by_core(2, -by)) for by in (1, 2, 3)]
    wide = jnp.pad(cells, ((0, 0),) * 3 + ((0, 2), (0, 0)))
    own = lax.dynamic_slice_in_dim(wide, 3 * xhi, 5, 1).reshape(2560, 128)
    across = send(lax.dynamic_slice_in_dim(wide, 3 * (1 - xhi), 5, 1).reshape(2560, 128), ACROSS)
    own_there = send(own, CORES)

    def edge(column):
        return jnp.concatenate([above[:, :, None, column], cells[:, :, :, column], below[:, :, None, column]], axis=2)

    left, right = send(edge(29), column_step(1)), send(edge(0), column_step(-1))
    shard, left, right = lax.optimization_barrier((jnp.stack(near), left, right))
    weights = [shard] + [send(shard, around_by_core(1, -by)) for by in (1, 2, 3)]
    own_rim, other_rim = pack_rims(position, above, below, left, right)
    across_rim = send(other_rim, ACROSS)
    across, across_rim, weights[2] = lax.optimization_barrier((across, across_rim, weights[2]))
    rims = [own_rim, send(own_rim, CORES), across_rim, send(across_rim, CORES)]
    mains = [own, own_there, across, send(across, CORES)]
    by_frame = [sum(row[i] * taps[i] for i in range(3) if row[i]) for row in TAPS]
    by_frame = jnp.stack(by_frame).reshape(6, 3, 3, 2, 8, 128)
    by_row = [sum(row[j] * by_frame[:, j] for j in range(3) if row[j]) for row in ROW_TAPS]
    taps = jnp.stack(by_row, axis=1).reshape(6, 12, 2, 8, 128)
    taps = taps * jnp.array([1.0, 0.5], F32)[None, None, :, None, None]

    kept, sent = run_block(position, pack_cells(position, mains, rims), weights, taps)
    total = kept + send(sent, CORES).astype(F32)
    return total[:, :, None, :, :30].astype(BF16)


def solution(mesh):
    return jax.shard_map(
        on_device,
        mesh=mesh,
        in_specs=(
            P(None, None, "tile", None, None, "ch"),
            P("tile", None, "ch"),
            P(None, None, None, None, "ch"),
            P("ch", "tile"),
        ),
        out_specs=P(None, "ch", "tile", None, None, None),
        check_vma=False,
    )
```

```python
import functools

import jax
import jax.numpy as jnp
from jax import lax
from jax.experimental import pallas as pl
from jax.experimental.pallas import tpu as pltpu
from jax.sharding import PartitionSpec as P

F32 = jnp.float32
BF16 = jnp.bfloat16
BOTH = ("ch", "tile")


def device_pairs(move):
    pairs = []
    for ch in range(4):
        for tile in range(32):
            x, core = (ch // 2) * 2 + (tile // 4) % 2, ch % 2
            y, z = tile // 8, tile % 4
            to = move(x, y, z, core)
            if to is not None:
                tx, ty, tz, tc = to
                target = ((tx // 2) * 2 + tc) * 32 + (ty * 2 + tx % 2) * 4 + tz
                pairs.append((ch * 32 + tile, target))
    return pairs


def around(axis, by):
    def move(x, y, z, core):
        at = [x, y, z]
        at[axis] = (at[axis] + by) % 4
        return (*at, core)

    return device_pairs(move)


def around_by_core(first, by):
    def move(x, y, z, core):
        at = [x, y, z]
        at[first if core == 0 else 3 - first] = (at[first if core == 0 else 3 - first] + by) % 4
        return (*at, core)

    return device_pairs(move)


def column_step(by):
    def move(x, y, z, core):
        return (x, y, z + by, core) if 0 <= z + by < 4 else None

    return device_pairs(move)


def row_step(by):
    def move(x, y, z, core):
        row = y * 2 + x % 2 + by
        return ((x // 2) * 2 + row % 2, row // 2, z, core) if 0 <= row < 8 else None

    return device_pairs(move)


ACROSS = around(0, 2)
BESIDE = device_pairs(lambda x, y, z, core: (x ^ 1, y, z, core))
DIAGONAL = device_pairs(lambda x, y, z, core: (x ^ 3, y, z, core))
CORES = device_pairs(lambda x, y, z, core: (x, y, z, 1 - core))


def send(value, pairs):
    return lax.ppermute(value, BOTH, pairs)


def forward(frames):
    d1, d2, d3, d4, d5 = frames
    a, b = d4 - 4.0 * d2, d3 - 4.0 * d1
    c, e = d4 - d2, d3 - d1
    e = e + e
    return a - d2, a + b, a - b, c + e, c - e, d5 - d3 - (e + e)


def backward(m):
    p, q, r, s = m[1] + m[2], m[1] - m[2], m[3] + m[4], m[3] - m[4]
    s = s + s
    return m[0] + p + r, q + s, p + 4.0 * r, q + 4.0 * s + m[5]


TAPS = (
    (1 / 4, 0, 0),
    (-1 / 6, -1 / 6, -1 / 6),
    (-1 / 6, 1 / 6, -1 / 6),
    (1 / 24, 1 / 12, 1 / 6),
    (1 / 24, -1 / 12, 1 / 6),
    (0, 0, 1),
)


ROW_TAPS = ((1, 0, 0), (1 / 2, 1 / 2, 1 / 2), (1 / 2, -1 / 2, 1 / 2), (0, 0, 1))


def from_left(x):
    return jnp.concatenate([pltpu.roll(x[24:32], 1, 0), x[0:24]], axis=0)


def from_right(x):
    return jnp.concatenate([x[8:32], pltpu.roll(x[0:8], 7, 0)], axis=0)


def rim_kernel(pos_ref, above, below, left, right, own_ref, other_ref, tile, edge):
    xhi = pos_ref[0]

    def one(i, _):
        for out, start in ((own_ref, 3 * xhi), (other_ref, 3 * (1 - xhi))):
            b, f = i // 5, start + i % 5
            tile[0:30, :] = above[b, f].astype(F32)
            tile[32:62, :] = below[b, f].astype(F32)
            for k, side in enumerate((right, left)):
                edge[k, 0:10, :] = side[b, f].astype(F32)
                tile[30 + k:31 + k, :] = edge[k, 0:1, :]
                tile[62 + k:63 + k, :] = edge[k, 9:10, :]
                tile[64 + 8 * k:72 + 8 * k, :] = edge[k, 1:9, :]
            out[pl.ds(pl.multiple_of(i * 80, 16), 80), :] = tile[...].astype(BF16)
        return 0

    lax.fori_loop(0, 10, one, 0)


def pack_rims(position, above, below, left, right):
    vmem = pl.BlockSpec(memory_space=pltpu.VMEM)
    return pl.pallas_call(
        rim_kernel,
        out_shape=[jax.ShapeDtypeStruct((800, 128), BF16)] * 2,
        in_specs=[pl.BlockSpec(memory_space=pltpu.SMEM)] + [vmem] * 4,
        out_specs=[vmem] * 2,
        scratch_shapes=[pltpu.VMEM((80, 128), F32), pltpu.VMEM((2, 16, 128), F32)],
        compiler_params=pltpu.CompilerParams(vmem_limit_bytes=16 * 2**20),
        name="pack_rims",
    )(position, above, below, left, right)


def pack_kernel(pos_ref, m0, m1, m2, m3, r0, r1, r2, r3, x_ref, rows):
    xhi = pos_ref[0]
    ch = xhi * 2 + pos_ref[1]
    mains, rims = (m0, m1, m2, m3), (r0, r1, r2, r3)

    def one(i, _):
        b, f = i // 5, i % 5
        to = jnp.where(xhi == 1, 4 - f, f)
        for r, (main, rim) in enumerate(zip(mains, rims)):
            strips = rim[pl.ds(pl.multiple_of(i * 80, 16), 80), :].astype(F32)
            rows[r, 0:32, :] = strips[0:32]
            rows[r, 288:320, :] = strips[32:64]
            for h in range(8):
                at = pl.ds(pl.multiple_of(i * 256 + h * 32, 32), 32)
                rows[r, (h + 1) * 32:(h + 2) * 32, :] = main[at, :].astype(F32)
            rows[r, pl.ds(62, 8, stride=32), :] = strips[64:72]
            rows[r, pl.ds(63, 8, stride=32), :] = strips[72:80]
            for h in range(10):
                tile = jnp.concatenate([rows[r, pl.ds(h * 32 + q, 8, stride=4), :] for q in range(4)], axis=0)
                x_ref[ch ^ r, b, pl.ds(pl.multiple_of((h * 5 + to) * 32, 32), 32), :] = tile.astype(BF16)
        return 0

    lax.fori_loop(0, 10, one, 0)


def pack_cells(position, mains, rims):
    vmem = pl.BlockSpec(memory_space=pltpu.VMEM)
    return pl.pallas_call(
        pack_kernel,
        out_shape=jax.ShapeDtypeStruct((4, 2, 1600, 128), BF16),
        in_specs=[pl.BlockSpec(memory_space=pltpu.SMEM)] + [vmem] * 8,
        out_specs=vmem,
        scratch_shapes=[pltpu.VMEM((4, 320, 128), F32)],
        compiler_params=pltpu.CompilerParams(vmem_limit_bytes=16 * 2**20),
        name="pack_cells",
    )(position, *mains, *rims)


def block_kernel(pos_ref, x_ref, p0, p1, p2, p3, k_ref, kept_ref, sent_ref,
                 w_scr, wp_scr, t0, t1, hidden, acc, rows):
    xhi, core, y, z, xlo = (pos_ref[i] for i in range(5))
    for r, piece in enumerate((p0, p1, p2, p3)):
        for o in range(4):
            py = jnp.where(core == 0, y + r, y + o) % 4
            pz = jnp.where(core == 0, z + o, z + r) % 4
            for p in range(2):
                row = pl.ds(pl.multiple_of(((py * 2 + (xlo ^ p)) * 4 + pz) * 16, 16), 16)
                for half in range(2):
                    for g in range(2):
                        w_scr[g, half, row, :] = piece[o, half, p, g]
                    wp_scr[row, half * 512:(half + 1) * 512] = piece[o, half, p, 2]

    def weights(g, c):
        return w_scr[g, c // 2, :, pl.ds(pl.multiple_of((c % 2) * 256, 256), 256)]

    def expand(s, row, g, t):
        b, c = s // 4, s % 4
        at = pl.ds(pl.multiple_of(row * 160, 32), 160)
        cells = jnp.concatenate([x_ref[m, b, at, :] for m in range(4)], axis=1)
        half = jnp.dot(cells, weights(g, c), preferred_element_type=F32)
        half = half * jnp.tanh(half) + half
        for q in range(2):
            frames = [half[f * 32:(f + 1) * 32, q * 128:(q + 1) * 128] for f in range(5)]
            for m, v in enumerate(forward(frames)):
                t[g * 2 + q, m, row] = v

    def filtered(t, group, g, tap, h):
        terms = [[], []]
        for m in range(6):
            d = [t[group, m, h + i] for i in range(4)]
            d = [d[0] - d[2], d[1] + d[2], d[2] - d[1], d[1] - d[3]]
            p = []
            for i in range(4):
                x = [d[i] * k_ref[m, i * 3 + l, g, pl.ds(tap, 1), :] for l in range(3)]
                p.append(x[1] + from_left(x[0]) + from_right(x[2]))
            terms[0].append(p[0] + p[1] + p[2])
            terms[1].append(p[1] - p[2] - p[3])
        return [backward(m) for m in terms]

    def gate_rows(t, c, h):
        for q in range(2):
            value = filtered(t, q, 0, c * 2 + q, h)
            gate = filtered(t, 2 + q, 1, c * 2 + q, h)
            for r in range(2):
                both = [(v * (u * jnp.tanh(u) + u)).astype(BF16) for v, u in zip(value[r], gate[r])]
                at = pl.ds(pl.multiple_of((h + r) * 128, 128), 128)
                hidden[c, at, q * 128:(q + 1) * 128] = jnp.concatenate(both, axis=0)

    def project(b):
        def part(i, _):
            at = pl.ds(pl.multiple_of(i * 512, 512), 512)
            units = jnp.concatenate([hidden[c, at, :] for c in range(4)], axis=1)
            new = lax.dot_general(units, wp_scr[...], (((1,), (1,)), ((), ())), preferred_element_type=F32)
            acc[b, at, :] = new
            return 0

        lax.fori_loop(0, 2, part, 0)

    def first(row, _):
        for g in range(2):
            expand(0, row, g, t0)
        return 0

    lax.fori_loop(0, 10, first, 0)

    def step(s, now, later):
        def half(it, _):
            for r in range(2):
                gate_rows(now, s % 4, it * 4 + 2 * r)
                if later is not None:
                    for u in range(5):
                        expand(s + 1, it * 5 + u, r, later)
            return 0

        lax.fori_loop(0, 2, half, 0)

    def pair(i, _):
        step(2 * i, t0, t1)
        step(2 * i + 1, t1, t0)

        @pl.when(i == 1)
        def _():
            project(0)

        return 0

    lax.fori_loop(0, 3, pair, 0)
    step(6, t0, t1)
    step(7, t1, None)
    project(1)

    def move(i, _):
        for u in range(8):
            b, f, h = i // 2, i % 2, u
            for slot in range(2):
                true = (core ^ slot) * 2 + f
                frame = jnp.where(xhi == 1, 3 - true, true)
                at = pl.ds(pl.multiple_of((h * 4 + frame) * 32, 32), 32)
                total = acc[b, at, :]
                if slot == 0:
                    cells_at = pl.ds(pl.multiple_of(((h + 1) * 5 + frame) * 32, 32), 32)
                    cells = jnp.concatenate([x_ref[m, b, cells_at, :] for m in range(4)], axis=1)
                    total = total + cells.astype(F32)
                own = u * 8 + slot * 4
                for v in range(4):
                    for q in range(4):
                        rows[own + v, pl.ds(q, 8, stride=4), :] = total[q * 8:(q + 1) * 8, v * 128:(v + 1) * 128]
        for u in range(8):
            for slot, out in ((0, kept_ref), (1, sent_ref)):
                own = u * 8 + slot * 4
                total = jnp.concatenate([rows[own + v] for v in range(4)], axis=1)
                out[i // 2, i % 2, u] = total.astype(out.dtype)
        return 0

    lax.fori_loop(0, 4, move, 0)


def run_block(position, cells, weights, taps):
    vmem = pl.BlockSpec(memory_space=pltpu.VMEM)
    return pl.pallas_call(
        block_kernel,
        out_shape=[jax.ShapeDtypeStruct((2, 2, 8, 32, 512), t) for t in (F32, BF16)],
        in_specs=[pl.BlockSpec(memory_space=pltpu.SMEM)] + [vmem] * 6,
        out_specs=[vmem] * 2,
        scratch_shapes=[
            pltpu.VMEM((2, 2, 512, 512), BF16),
            pltpu.VMEM((512, 1024), BF16),
            pltpu.VMEM((4, 6, 10, 32, 128), F32),
            pltpu.VMEM((4, 6, 10, 32, 128), F32),
            pltpu.VMEM((4, 1024, 256), BF16),
            pltpu.VMEM((2, 1024, 512), F32),
            pltpu.VMEM((64, 32, 128), F32),
        ],
        compiler_params=pltpu.CompilerParams(vmem_limit_bytes=32 * 2**20),
        name="gated_block",
    )(position, cells, *weights, taps)


def on_device(latent, expand_weight, depth_kernel, project_weight):
    ch, tile = lax.axis_index("ch"), lax.axis_index("tile")
    xhi, core = ch // 2, ch % 2
    y, xlo, z = tile // 8, (tile // 4) % 2, tile % 4
    position = jnp.stack([xhi, core, y, z, xlo]).astype(jnp.int32)
    cells = latent[:, :, 0]

    half = expand_weight * jnp.asarray(0.5, BF16)
    shard = jnp.stack([half[:, 0], half[:, 1], project_weight.T])
    taps = depth_kernel.reshape(3, 9, 2, 512)
    back = taps[::-1]
    there = jnp.where(xhi == 1, taps, back).astype(BF16).reshape(54, 512)
    taps = jnp.where(xhi == 1, back, taps)
    far = send(jnp.concatenate([shard.reshape(48, 512), there]), ACROSS)
    shard = jnp.stack([shard, send(shard, BESIDE), far[:48].reshape(3, 16, 512), send(shard, DIAGONAL)])
    shard = shard.reshape(2, 2, 3, 16, 512)
    taps = jnp.concatenate(
        [taps.reshape(3, 9, 2, 4, 128), far[48:].astype(F32).reshape(3, 9, 2, 4, 128)], axis=3)
    above = send(cells[:, :, 7], row_step(1))
    below = send(cells[:, :, 0], row_step(-1))

    shard, cells = lax.optimization_barrier((shard, cells))
    near = [shard] + [send(shard, around_by_core(2, -by)) for by in (1, 2, 3)]
    wide = jnp.pad(cells, ((0, 0),) * 3 + ((0, 2), (0, 0)))
    own = lax.dynamic_slice_in_dim(wide, 3 * xhi, 5, 1).reshape(2560, 128)
    across = send(lax.dynamic_slice_in_dim(wide, 3 * (1 - xhi), 5, 1).reshape(2560, 128), ACROSS)
    own_there = send(own, CORES)

    def edge(column):
        return jnp.concatenate([above[:, :, None, column], cells[:, :, :, column], below[:, :, None, column]], axis=2)

    left, right = send(edge(29), column_step(1)), send(edge(0), column_step(-1))
    shard, left, right, own_there = lax.optimization_barrier((jnp.stack(near), left, right, own_there))
    weights = [shard] + [send(shard, around_by_core(1, -by)) for by in (1, 2, 3)]
    own_rim, other_rim = pack_rims(position, above, below, left, right)
    across_rim = send(other_rim, ACROSS)
    across, across_rim, weights[2] = lax.optimization_barrier((across, across_rim, weights[2]))
    rims = [own_rim, send(own_rim, CORES), across_rim, send(across_rim, CORES)]
    mains = [own, own_there, across, send(across, CORES)]
    by_frame = [sum(row[i] * taps[i] for i in range(3) if row[i]) for row in TAPS]
    by_frame = jnp.stack(by_frame).reshape(6, 3, 3, 2, 8, 128)
    by_row = [sum(row[j] * by_frame[:, j] for j in range(3) if row[j]) for row in ROW_TAPS]
    taps = jnp.stack(by_row, axis=1).reshape(6, 12, 2, 8, 128)
    taps = taps * jnp.array([1.0, 0.5], F32)[None, None, :, None, None]

    kept, sent = run_block(position, pack_cells(position, mains, rims), weights, taps)
    total = kept + send(sent, CORES).astype(F32)
    return total[:, :, None, :, :30].astype(BF16)


def solution(mesh):
    return jax.shard_map(
        on_device,
        mesh=mesh,
        in_specs=(
            P(None, None, "tile", None, None, "ch"),
            P("tile", None, "ch"),
            P(None, None, None, None, "ch"),
            P("ch", "tile"),
        ),
        out_specs=P(None, "ch", "tile", None, None, None),
        check_vma=False,
    )
```

```python
import functools

import jax
import jax.numpy as jnp
from jax import lax
from jax.experimental import pallas as pl
from jax.experimental.pallas import tpu as pltpu
from jax.sharding import PartitionSpec as P

F32 = jnp.float32
BF16 = jnp.bfloat16
BOTH = ("ch", "tile")


def device_pairs(move):
    pairs = []
    for ch in range(4):
        for tile in range(32):
            x, core = (ch // 2) * 2 + (tile // 4) % 2, ch % 2
            y, z = tile // 8, tile % 4
            to = move(x, y, z, core)
            if to is not None:
                tx, ty, tz, tc = to
                target = ((tx // 2) * 2 + tc) * 32 + (ty * 2 + tx % 2) * 4 + tz
                pairs.append((ch * 32 + tile, target))
    return pairs


def around(axis, by):
    def move(x, y, z, core):
        at = [x, y, z]
        at[axis] = (at[axis] + by) % 4
        return (*at, core)

    return device_pairs(move)


def around_by_core(first, by):
    def move(x, y, z, core):
        at = [x, y, z]
        at[first if core == 0 else 3 - first] = (at[first if core == 0 else 3 - first] + by) % 4
        return (*at, core)

    return device_pairs(move)


def column_step(by):
    def move(x, y, z, core):
        return (x, y, z + by, core) if 0 <= z + by < 4 else None

    return device_pairs(move)


def row_step(by):
    def move(x, y, z, core):
        row = y * 2 + x % 2 + by
        return ((x // 2) * 2 + row % 2, row // 2, z, core) if 0 <= row < 8 else None

    return device_pairs(move)


ACROSS = around(0, 2)
BESIDE = device_pairs(lambda x, y, z, core: (x ^ 1, y, z, core))
DIAGONAL = device_pairs(lambda x, y, z, core: (x ^ 3, y, z, core))
CORES = device_pairs(lambda x, y, z, core: (x, y, z, 1 - core))


def send(value, pairs):
    return lax.ppermute(value, BOTH, pairs)


def forward(frames):
    d1, d2, d3, d4, d5 = frames
    a, b = d4 - 4.0 * d2, d3 - 4.0 * d1
    c, e = d4 - d2, d3 - d1
    e = e + e
    return a - d2, a + b, a - b, c + e, c - e, d5 - d3 - (e + e)


def backward(m):
    p, q, r, s = m[1] + m[2], m[1] - m[2], m[3] + m[4], m[3] - m[4]
    s = s + s
    return m[0] + p + r, q + s, p + 4.0 * r, q + 4.0 * s + m[5]


TAPS = (
    (1 / 4, 0, 0),
    (-1 / 6, -1 / 6, -1 / 6),
    (-1 / 6, 1 / 6, -1 / 6),
    (1 / 24, 1 / 12, 1 / 6),
    (1 / 24, -1 / 12, 1 / 6),
    (0, 0, 1),
)


ROW_TAPS = ((1, 0, 0), (1 / 2, 1 / 2, 1 / 2), (1 / 2, -1 / 2, 1 / 2), (0, 0, 1))


def from_left(x):
    return jnp.concatenate([pltpu.roll(x[24:32], 1, 0), x[0:24]], axis=0)


def from_right(x):
    return jnp.concatenate([x[8:32], pltpu.roll(x[0:8], 7, 0)], axis=0)


def rim_kernel(pos_ref, above, below, left, right, own_ref, other_ref, tile, edge):
    xhi = pos_ref[0]

    def one(i, _):
        for out, start in ((own_ref, 3 * xhi), (other_ref, 3 * (1 - xhi))):
            b, f = i // 5, start + i % 5
            tile[0:30, :] = above[b, f].astype(F32)
            tile[32:62, :] = below[b, f].astype(F32)
            for k, side in enumerate((right, left)):
                edge[k, 0:10, :] = side[b, f].astype(F32)
                tile[30 + k:31 + k, :] = edge[k, 0:1, :]
                tile[62 + k:63 + k, :] = edge[k, 9:10, :]
                tile[64 + 8 * k:72 + 8 * k, :] = edge[k, 1:9, :]
            out[pl.ds(pl.multiple_of(i * 80, 16), 80), :] = tile[...].astype(BF16)
        return 0

    lax.fori_loop(0, 10, one, 0)


def pack_rims(position, above, below, left, right):
    vmem = pl.BlockSpec(memory_space=pltpu.VMEM)
    return pl.pallas_call(
        rim_kernel,
        out_shape=[jax.ShapeDtypeStruct((800, 128), BF16)] * 2,
        in_specs=[pl.BlockSpec(memory_space=pltpu.SMEM)] + [vmem] * 4,
        out_specs=[vmem] * 2,
        scratch_shapes=[pltpu.VMEM((80, 128), F32), pltpu.VMEM((2, 16, 128), F32)],
        compiler_params=pltpu.CompilerParams(vmem_limit_bytes=16 * 2**20),
        name="pack_rims",
    )(position, above, below, left, right)


def pack_kernel(pos_ref, m0, m1, m2, m3, r0, r1, r2, r3, x_ref, rows):
    xhi = pos_ref[0]
    ch = xhi * 2 + pos_ref[1]
    mains, rims = (m0, m1, m2, m3), (r0, r1, r2, r3)

    def one(i, _):
        b, f = i // 5, i % 5
        to = jnp.where(xhi == 1, 4 - f, f)
        for r, (main, rim) in enumerate(zip(mains, rims)):
            strips = rim[pl.ds(pl.multiple_of(i * 80, 16), 80), :].astype(F32)
            rows[r, 0:32, :] = strips[0:32]
            rows[r, 288:320, :] = strips[32:64]
            for h in range(8):
                at = pl.ds(pl.multiple_of(i * 256 + h * 32, 32), 32)
                rows[r, (h + 1) * 32:(h + 2) * 32, :] = main[at, :].astype(F32)
            rows[r, pl.ds(62, 8, stride=32), :] = strips[64:72]
            rows[r, pl.ds(63, 8, stride=32), :] = strips[72:80]
            for h in range(10):
                tile = jnp.concatenate([rows[r, pl.ds(h * 32 + q, 8, stride=4), :] for q in range(4)], axis=0)
                x_ref[ch ^ r, b, pl.ds(pl.multiple_of((h * 5 + to) * 32, 32), 32), :] = tile.astype(BF16)
        return 0

    lax.fori_loop(0, 10, one, 0)


def pack_cells(position, mains, rims):
    vmem = pl.BlockSpec(memory_space=pltpu.VMEM)
    return pl.pallas_call(
        pack_kernel,
        out_shape=jax.ShapeDtypeStruct((4, 2, 1600, 128), BF16),
        in_specs=[pl.BlockSpec(memory_space=pltpu.SMEM)] + [vmem] * 8,
        out_specs=vmem,
        scratch_shapes=[pltpu.VMEM((4, 320, 128), F32)],
        compiler_params=pltpu.CompilerParams(vmem_limit_bytes=16 * 2**20),
        name="pack_cells",
    )(position, *mains, *rims)


def block_kernel(pos_ref, x_ref, p0, p1, p2, p3, k_ref, kept_ref, sent_ref,
                 w_scr, wp_scr, t0, t1, hidden, acc, rows):
    xhi, core, y, z, xlo = (pos_ref[i] for i in range(5))
    for r, piece in enumerate((p0, p1, p2, p3)):
        for o in range(4):
            py = jnp.where(core == 0, y + r, y + o) % 4
            pz = jnp.where(core == 0, z + o, z + r) % 4
            for p in range(2):
                row = pl.ds(pl.multiple_of(((py * 2 + (xlo ^ p)) * 4 + pz) * 16, 16), 16)
                for half in range(2):
                    for g in range(2):
                        w_scr[g, half, row, :] = piece[o, half, p, g]
                    wp_scr[row, half * 512:(half + 1) * 512] = piece[o, half, p, 2]

    def weights(g, c):
        return w_scr[g, c // 2, :, pl.ds(pl.multiple_of((c % 2) * 256, 256), 256)]

    def expand(s, row, g, t, count=1):
        b, c = s // 4, s % 4
        at = pl.ds(pl.multiple_of(row * 160, 32), count * 160)
        cells = jnp.concatenate([x_ref[m, b, at, :] for m in range(4)], axis=1)
        half = jnp.dot(cells, weights(g, c), preferred_element_type=F32)
        half = half * jnp.tanh(half) + half
        for k in range(count):
            for q in range(2):
                frames = [half[(k * 5 + f) * 32:(k * 5 + f + 1) * 32, q * 128:(q + 1) * 128] for f in range(5)]
                for m, v in enumerate(forward(frames)):
                    t[g * 2 + q, m, row + k] = v

    def filtered(t, group, g, tap, h):
        terms = [[], []]
        for m in range(6):
            d = [t[group, m, h + i] for i in range(4)]
            d = [d[0] - d[2], d[1] + d[2], d[2] - d[1], d[1] - d[3]]
            p = []
            for i in range(4):
                x = [d[i] * k_ref[m, i * 3 + l, g, pl.ds(tap, 1), :] for l in range(3)]
                p.append(x[1] + from_left(x[0]) + from_right(x[2]))
            terms[0].append(p[0] + p[1] + p[2])
            terms[1].append(p[1] - p[2] - p[3])
        return [backward(m) for m in terms]

    def gate_rows(t, c, h):
        for q in range(2):
            value = filtered(t, q, 0, c * 2 + q, h)
            gate = filtered(t, 2 + q, 1, c * 2 + q, h)
            for r in range(2):
                both = [(v * (u * jnp.tanh(u) + u)).astype(BF16) for v, u in zip(value[r], gate[r])]
                at = pl.ds(pl.multiple_of((h + r) * 128, 128), 128)
                hidden[c, at, q * 128:(q + 1) * 128] = jnp.concatenate(both, axis=0)

    def project(b):
        def part(i, _):
            at = pl.ds(pl.multiple_of(i * 512, 512), 512)
            units = jnp.concatenate([hidden[c, at, :] for c in range(4)], axis=1)
            new = lax.dot_general(units, wp_scr[...], (((1,), (1,)), ((), ())), preferred_element_type=F32)
            acc[b, at, :] = new
            return 0

        lax.fori_loop(0, 2, part, 0)

    def first(it, _):
        for g in range(2):
            expand(0, it * 5, g, t0, 5)
        return 0

    lax.fori_loop(0, 2, first, 0)

    def step(s, now, later):
        def half(it, _):
            for r in range(2):
                gate_rows(now, s % 4, it * 4 + 2 * r)
                if later is not None:
                    expand(s + 1, it * 5, r, later, 3)
                    expand(s + 1, it * 5 + 3, r, later, 2)
            return 0

        lax.fori_loop(0, 2, half, 0)

    def pair(i, _):
        step(2 * i, t0, t1)
        step(2 * i + 1, t1, t0)

        @pl.when(i == 1)
        def _():
            project(0)

        return 0

    lax.fori_loop(0, 3, pair, 0)
    step(6, t0, t1)
    step(7, t1, None)
    project(1)

    def move(i, _):
        for u in range(8):
            b, f, h = i // 2, i % 2, u
            for slot in range(2):
                true = (core ^ slot) * 2 + f
                frame = jnp.where(xhi == 1, 3 - true, true)
                at = pl.ds(pl.multiple_of((h * 4 + frame) * 32, 32), 32)
                total = acc[b, at, :]
                if slot == 0:
                    cells_at = pl.ds(pl.multiple_of(((h + 1) * 5 + frame) * 32, 32), 32)
                    cells = jnp.concatenate([x_ref[m, b, cells_at, :] for m in range(4)], axis=1)
                    total = total + cells.astype(F32)
                own = u * 8 + slot * 4
                for v in range(4):
                    for q in range(4):
                        rows[own + v, pl.ds(q, 8, stride=4), :] = total[q * 8:(q + 1) * 8, v * 128:(v + 1) * 128]
        for u in range(8):
            for slot, out in ((0, kept_ref), (1, sent_ref)):
                own = u * 8 + slot * 4
                total = jnp.concatenate([rows[own + v] for v in range(4)], axis=1)
                out[i // 2, i % 2, u] = total.astype(out.dtype)
        return 0

    lax.fori_loop(0, 4, move, 0)


def run_block(position, cells, weights, taps):
    vmem = pl.BlockSpec(memory_space=pltpu.VMEM)
    return pl.pallas_call(
        block_kernel,
        out_shape=[jax.ShapeDtypeStruct((2, 2, 8, 32, 512), t) for t in (F32, BF16)],
        in_specs=[pl.BlockSpec(memory_space=pltpu.SMEM)] + [vmem] * 6,
        out_specs=[vmem] * 2,
        scratch_shapes=[
            pltpu.VMEM((2, 2, 512, 512), BF16),
            pltpu.VMEM((512, 1024), BF16),
            pltpu.VMEM((4, 6, 10, 32, 128), F32),
            pltpu.VMEM((4, 6, 10, 32, 128), F32),
            pltpu.VMEM((4, 1024, 256), BF16),
            pltpu.VMEM((2, 1024, 512), F32),
            pltpu.VMEM((64, 32, 128), F32),
        ],
        compiler_params=pltpu.CompilerParams(vmem_limit_bytes=32 * 2**20),
        name="gated_block",
    )(position, cells, *weights, taps)


def on_device(latent, expand_weight, depth_kernel, project_weight):
    ch, tile = lax.axis_index("ch"), lax.axis_index("tile")
    xhi, core = ch // 2, ch % 2
    y, xlo, z = tile // 8, (tile // 4) % 2, tile % 4
    position = jnp.stack([xhi, core, y, z, xlo]).astype(jnp.int32)
    cells = latent[:, :, 0]

    half = expand_weight * jnp.asarray(0.5, BF16)
    shard = jnp.stack([half[:, 0], half[:, 1], project_weight.T])
    taps = depth_kernel.reshape(3, 9, 2, 512)
    back = taps[::-1]
    there = jnp.where(xhi == 1, taps, back).astype(BF16).reshape(54, 512)
    taps = jnp.where(xhi == 1, back, taps)
    far = send(jnp.concatenate([shard.reshape(48, 512), there]), ACROSS)
    shard = jnp.stack([shard, send(shard, BESIDE), far[:48].reshape(3, 16, 512), send(shard, DIAGONAL)])
    shard = shard.reshape(2, 2, 3, 16, 512)
    taps = jnp.concatenate(
        [taps.reshape(3, 9, 2, 4, 128), far[48:].astype(F32).reshape(3, 9, 2, 4, 128)], axis=3)
    above = send(cells[:, :, 7], row_step(1))
    below = send(cells[:, :, 0], row_step(-1))

    shard, cells = lax.optimization_barrier((shard, cells))
    near = [shard] + [send(shard, around_by_core(2, -by)) for by in (1, 2, 3)]
    wide = jnp.pad(cells, ((0, 0),) * 3 + ((0, 2), (0, 0)))
    own = lax.dynamic_slice_in_dim(wide, 3 * xhi, 5, 1).reshape(2560, 128)
    across = send(lax.dynamic_slice_in_dim(wide, 3 * (1 - xhi), 5, 1).reshape(2560, 128), ACROSS)
    own_there = send(own, CORES)

    def edge(column):
        return jnp.concatenate([above[:, :, None, column], cells[:, :, :, column], below[:, :, None, column]], axis=2)

    left, right = send(edge(29), column_step(1)), send(edge(0), column_step(-1))
    shard, left, right, own_there = lax.optimization_barrier((jnp.stack(near), left, right, own_there))
    weights = [shard] + [send(shard, around_by_core(1, -by)) for by in (1, 2, 3)]
    own_rim, other_rim = pack_rims(position, above, below, left, right)
    across_rim = send(other_rim, ACROSS)
    across, across_rim, weights[2] = lax.optimization_barrier((across, across_rim, weights[2]))
    rims = [own_rim, send(own_rim, CORES), across_rim, send(across_rim, CORES)]
    mains = [own, own_there, across, send(across, CORES)]
    by_frame = [sum(row[i] * taps[i] for i in range(3) if row[i]) for row in TAPS]
    by_frame = jnp.stack(by_frame).reshape(6, 3, 3, 2, 8, 128)
    by_row = [sum(row[j] * by_frame[:, j] for j in range(3) if row[j]) for row in ROW_TAPS]
    taps = jnp.stack(by_row, axis=1).reshape(6, 12, 2, 8, 128)
    taps = taps * jnp.array([1.0, 0.5], F32)[None, None, :, None, None]

    kept, sent = run_block(position, pack_cells(position, mains, rims), weights, taps)
    total = kept + send(sent, CORES).astype(F32)
    return total[:, :, None, :, :30].astype(BF16)


def solution(mesh):
    return jax.shard_map(
        on_device,
        mesh=mesh,
        in_specs=(
            P(None, None, "tile", None, None, "ch"),
            P("tile", None, "ch"),
            P(None, None, None, None, "ch"),
            P("ch", "tile"),
        ),
        out_specs=P(None, "ch", "tile", None, None, None),
        check_vma=False,
    )
```

```python
import functools

import jax
import jax.numpy as jnp
from jax import lax
from jax.experimental import pallas as pl
from jax.experimental.pallas import tpu as pltpu
from jax.sharding import PartitionSpec as P

F32 = jnp.float32
BF16 = jnp.bfloat16
BOTH = ("ch", "tile")


def device_pairs(move):
    pairs = []
    for ch in range(4):
        for tile in range(32):
            x, core = (ch // 2) * 2 + (tile // 4) % 2, ch % 2
            y, z = tile // 8, tile % 4
            to = move(x, y, z, core)
            if to is not None:
                tx, ty, tz, tc = to
                target = ((tx // 2) * 2 + tc) * 32 + (ty * 2 + tx % 2) * 4 + tz
                pairs.append((ch * 32 + tile, target))
    return pairs


def around(axis, by):
    def move(x, y, z, core):
        at = [x, y, z]
        at[axis] = (at[axis] + by) % 4
        return (*at, core)

    return device_pairs(move)


def around_by_core(first, by):
    def move(x, y, z, core):
        at = [x, y, z]
        at[first if core == 0 else 3 - first] = (at[first if core == 0 else 3 - first] + by) % 4
        return (*at, core)

    return device_pairs(move)


def column_step(by):
    def move(x, y, z, core):
        return (x, y, z + by, core) if 0 <= z + by < 4 else None

    return device_pairs(move)


def row_step(by):
    def move(x, y, z, core):
        row = y * 2 + x % 2 + by
        return ((x // 2) * 2 + row % 2, row // 2, z, core) if 0 <= row < 8 else None

    return device_pairs(move)


ACROSS = around(0, 2)
BESIDE = device_pairs(lambda x, y, z, core: (x ^ 1, y, z, core))
DIAGONAL = device_pairs(lambda x, y, z, core: (x ^ 3, y, z, core))
CORES = device_pairs(lambda x, y, z, core: (x, y, z, 1 - core))


def send(value, pairs):
    return lax.ppermute(value, BOTH, pairs)


def forward(frames):
    d1, d2, d3, d4, d5 = frames
    a, b = d4 - 4.0 * d2, d3 - 4.0 * d1
    c, e = d4 - d2, d3 - d1
    e = e + e
    return a - d2, a + b, a - b, c + e, c - e, d5 - d3 - (e + e)


def backward(m):
    p, q, r, s = m[1] + m[2], m[1] - m[2], m[3] + m[4], m[3] - m[4]
    s = s + s
    return m[0] + p + r, q + s, p + 4.0 * r, q + 4.0 * s + m[5]


TAPS = (
    (1 / 4, 0, 0),
    (-1 / 6, -1 / 6, -1 / 6),
    (-1 / 6, 1 / 6, -1 / 6),
    (1 / 24, 1 / 12, 1 / 6),
    (1 / 24, -1 / 12, 1 / 6),
    (0, 0, 1),
)


ROW_TAPS = ((1, 0, 0), (1 / 2, 1 / 2, 1 / 2), (1 / 2, -1 / 2, 1 / 2), (0, 0, 1))


def from_left(x):
    return jnp.concatenate([pltpu.roll(x[24:32], 1, 0), x[0:24]], axis=0)


def from_right(x):
    return jnp.concatenate([x[8:32], pltpu.roll(x[0:8], 7, 0)], axis=0)


def rim_kernel(pos_ref, above, below, left, right, own_ref, other_ref, tile, edge):
    xhi = pos_ref[0]

    def one(i, _):
        for out, start in ((own_ref, 3 * xhi), (other_ref, 3 * (1 - xhi))):
            b, f = i // 5, start + i % 5
            tile[0:30, :] = above[b, f].astype(F32)
            tile[32:62, :] = below[b, f].astype(F32)
            for k, side in enumerate((right, left)):
                edge[k, 0:10, :] = side[b, f].astype(F32)
                tile[30 + k:31 + k, :] = edge[k, 0:1, :]
                tile[62 + k:63 + k, :] = edge[k, 9:10, :]
                tile[64 + 8 * k:72 + 8 * k, :] = edge[k, 1:9, :]
            out[pl.ds(pl.multiple_of(i * 80, 16), 80), :] = tile[...].astype(BF16)
        return 0

    lax.fori_loop(0, 10, one, 0)


def pack_rims(position, above, below, left, right):
    vmem = pl.BlockSpec(memory_space=pltpu.VMEM)
    return pl.pallas_call(
        rim_kernel,
        out_shape=[jax.ShapeDtypeStruct((800, 128), BF16)] * 2,
        in_specs=[pl.BlockSpec(memory_space=pltpu.SMEM)] + [vmem] * 4,
        out_specs=[vmem] * 2,
        scratch_shapes=[pltpu.VMEM((80, 128), F32), pltpu.VMEM((2, 16, 128), F32)],
        compiler_params=pltpu.CompilerParams(vmem_limit_bytes=16 * 2**20),
        name="pack_rims",
    )(position, above, below, left, right)


def pack_kernel(pos_ref, m0, m1, m2, m3, r0, r1, r2, r3, x_ref, rows):
    xhi = pos_ref[0]
    ch = xhi * 2 + pos_ref[1]
    mains, rims = (m0, m1, m2, m3), (r0, r1, r2, r3)

    def one(i, _):
        b, f = i // 5, i % 5
        to = jnp.where(xhi == 1, 4 - f, f)
        for r, (main, rim) in enumerate(zip(mains, rims)):
            strips = rim[pl.ds(pl.multiple_of(i * 80, 16), 80), :].astype(F32)
            rows[r, 0:32, :] = strips[0:32]
            rows[r, 288:320, :] = strips[32:64]
            for h in range(8):
                at = pl.ds(pl.multiple_of(i * 256 + h * 32, 32), 32)
                rows[r, (h + 1) * 32:(h + 2) * 32, :] = main[at, :].astype(F32)
            rows[r, pl.ds(62, 8, stride=32), :] = strips[64:72]
            rows[r, pl.ds(63, 8, stride=32), :] = strips[72:80]
            for h in range(10):
                tile = jnp.concatenate([rows[r, pl.ds(h * 32 + q, 8, stride=4), :] for q in range(4)], axis=0)
                x_ref[ch ^ r, b, pl.ds(pl.multiple_of((h * 5 + to) * 32, 32), 32), :] = tile.astype(BF16)
        return 0

    lax.fori_loop(0, 10, one, 0)


def pack_cells(position, mains, rims):
    vmem = pl.BlockSpec(memory_space=pltpu.VMEM)
    return pl.pallas_call(
        pack_kernel,
        out_shape=jax.ShapeDtypeStruct((4, 2, 1600, 128), BF16),
        in_specs=[pl.BlockSpec(memory_space=pltpu.SMEM)] + [vmem] * 8,
        out_specs=vmem,
        scratch_shapes=[pltpu.VMEM((4, 328, 128), F32)],
        compiler_params=pltpu.CompilerParams(vmem_limit_bytes=16 * 2**20),
        name="pack_cells",
    )(position, *mains, *rims)


def block_kernel(pos_ref, x_ref, p0, p1, p2, p3, k_ref, kept_ref, sent_ref,
                 w_scr, wp_scr, t0, t1, hidden, acc, rows):
    xhi, core, y, z, xlo = (pos_ref[i] for i in range(5))
    for r, piece in enumerate((p0, p1, p2, p3)):
        for o in range(4):
            py = jnp.where(core == 0, y + r, y + o) % 4
            pz = jnp.where(core == 0, z + o, z + r) % 4
            for p in range(2):
                row = pl.ds(pl.multiple_of(((py * 2 + (xlo ^ p)) * 4 + pz) * 16, 16), 16)
                for half in range(2):
                    for g in range(2):
                        w_scr[g, half, row, :] = piece[o, half, p, g]
                    wp_scr[row, half * 512:(half + 1) * 512] = piece[o, half, p, 2]

    def weights(g, c):
        return w_scr[g, c // 2, :, pl.ds(pl.multiple_of((c % 2) * 256, 256), 256)]

    def expand(s, row, g, t, count=1):
        b, c = s // 4, s % 4
        at = pl.ds(pl.multiple_of(row * 160, 32), count * 160)
        cells = jnp.concatenate([x_ref[m, b, at, :] for m in range(4)], axis=1)
        half = jnp.dot(cells, weights(g, c), preferred_element_type=F32)
        half = half * jnp.tanh(half) + half
        for k in range(count):
            for q in range(2):
                frames = [half[(k * 5 + f) * 32:(k * 5 + f + 1) * 32, q * 128:(q + 1) * 128] for f in range(5)]
                for m, v in enumerate(forward(frames)):
                    t[g * 2 + q, m, row + k] = v

    def filtered(t, group, g, tap, h):
        terms = [[], []]
        for m in range(6):
            d = [t[group, m, h + i] for i in range(4)]
            d = [d[0] - d[2], d[1] + d[2], d[2] - d[1], d[1] - d[3]]
            p = []
            for i in range(4):
                x = [d[i] * k_ref[m, i * 3 + l, g, pl.ds(tap, 1), :] for l in range(3)]
                p.append(x[1] + from_left(x[0]) + from_right(x[2]))
            terms[0].append(p[0] + p[1] + p[2])
            terms[1].append(p[1] - p[2] - p[3])
        return [backward(m) for m in terms]

    def gate_rows(t, c, h):
        for q in range(2):
            value = filtered(t, q, 0, c * 2 + q, h)
            gate = filtered(t, 2 + q, 1, c * 2 + q, h)
            for r in range(2):
                both = [(v * (u * jnp.tanh(u) + u)).astype(BF16) for v, u in zip(value[r], gate[r])]
                at = pl.ds(pl.multiple_of((h + r) * 128, 128), 128)
                hidden[c, at, q * 128:(q + 1) * 128] = jnp.concatenate(both, axis=0)

    def project(b):
        def part(i, _):
            at = pl.ds(pl.multiple_of(i * 512, 512), 512)
            units = jnp.concatenate([hidden[c, at, :] for c in range(4)], axis=1)
            new = lax.dot_general(units, wp_scr[...], (((1,), (1,)), ((), ())), preferred_element_type=F32)
            acc[b, at, :] = new
            return 0

        lax.fori_loop(0, 2, part, 0)

    def first(it, _):
        for g in range(2):
            expand(0, it * 5, g, t0, 5)
        return 0

    lax.fori_loop(0, 2, first, 0)

    def step(s, now, later):
        def half(it, _):
            for r in range(2):
                gate_rows(now, s % 4, it * 4 + 2 * r)
                if later is not None:
                    expand(s + 1, it * 5, r, later, 3)
                    expand(s + 1, it * 5 + 3, r, later, 2)
            return 0

        lax.fori_loop(0, 2, half, 0)

    def pair(i, _):
        step(2 * i, t0, t1)
        step(2 * i + 1, t1, t0)

        @pl.when(i == 1)
        def _():
            project(0)

        return 0

    lax.fori_loop(0, 3, pair, 0)
    step(6, t0, t1)
    step(7, t1, None)
    project(1)

    def move(i, _):
        for u in range(8):
            b, f, h = i // 2, i % 2, u
            for slot in range(2):
                true = (core ^ slot) * 2 + f
                frame = jnp.where(xhi == 1, 3 - true, true)
                at = pl.ds(pl.multiple_of((h * 4 + frame) * 32, 32), 32)
                total = acc[b, at, :]
                if slot == 0:
                    cells_at = pl.ds(pl.multiple_of(((h + 1) * 5 + frame) * 32, 32), 32)
                    cells = jnp.concatenate([x_ref[m, b, cells_at, :] for m in range(4)], axis=1)
                    total = total + cells.astype(F32)
                own = u * 8 + slot * 4
                for v in range(4):
                    for q in range(4):
                        rows[own + v, pl.ds(q, 8, stride=4), :] = total[q * 8:(q + 1) * 8, v * 128:(v + 1) * 128]
        for u in range(8):
            for slot, out in ((0, kept_ref), (1, sent_ref)):
                own = u * 8 + slot * 4
                total = jnp.concatenate([rows[own + v, 0:32, :] for v in range(4)], axis=1)
                out[i // 2, i % 2, u] = total.astype(out.dtype)
        return 0

    lax.fori_loop(0, 4, move, 0)


def run_block(position, cells, weights, taps):
    vmem = pl.BlockSpec(memory_space=pltpu.VMEM)
    return pl.pallas_call(
        block_kernel,
        out_shape=[jax.ShapeDtypeStruct((2, 2, 8, 32, 512), t) for t in (F32, BF16)],
        in_specs=[pl.BlockSpec(memory_space=pltpu.SMEM)] + [vmem] * 6,
        out_specs=[vmem] * 2,
        scratch_shapes=[
            pltpu.VMEM((2, 2, 512, 512), BF16),
            pltpu.VMEM((512, 1024), BF16),
            pltpu.VMEM((4, 6, 10, 32, 128), F32),
            pltpu.VMEM((4, 6, 10, 32, 128), F32),
            pltpu.VMEM((4, 1024, 256), BF16),
            pltpu.VMEM((2, 1024, 512), F32),
            pltpu.VMEM((64, 40, 128), F32),
        ],
        compiler_params=pltpu.CompilerParams(vmem_limit_bytes=32 * 2**20),
        name="gated_block",
    )(position, cells, *weights, taps)


def on_device(latent, expand_weight, depth_kernel, project_weight):
    ch, tile = lax.axis_index("ch"), lax.axis_index("tile")
    xhi, core = ch // 2, ch % 2
    y, xlo, z = tile // 8, (tile // 4) % 2, tile % 4
    position = jnp.stack([xhi, core, y, z, xlo]).astype(jnp.int32)
    cells = latent[:, :, 0]

    half = expand_weight * jnp.asarray(0.5, BF16)
    shard = jnp.stack([half[:, 0], half[:, 1], project_weight.T])
    taps = depth_kernel.reshape(3, 9, 2, 512)
    back = taps[::-1]
    there = jnp.where(xhi == 1, taps, back).astype(BF16).reshape(54, 512)
    taps = jnp.where(xhi == 1, back, taps)
    far = send(jnp.concatenate([shard.reshape(48, 512), there]), ACROSS)
    shard = jnp.stack([shard, send(shard, BESIDE), far[:48].reshape(3, 16, 512), send(shard, DIAGONAL)])
    shard = shard.reshape(2, 2, 3, 16, 512)
    taps = jnp.concatenate(
        [taps.reshape(3, 9, 2, 4, 128), far[48:].astype(F32).reshape(3, 9, 2, 4, 128)], axis=3)
    above = send(cells[:, :, 7], row_step(1))
    below = send(cells[:, :, 0], row_step(-1))

    shard, cells = lax.optimization_barrier((shard, cells))
    near = [shard] + [send(shard, around_by_core(2, -by)) for by in (1, 2, 3)]
    wide = jnp.pad(cells, ((0, 0),) * 3 + ((0, 2), (0, 0)))
    own = lax.dynamic_slice_in_dim(wide, 3 * xhi, 5, 1).reshape(2560, 128)
    across = send(lax.dynamic_slice_in_dim(wide, 3 * (1 - xhi), 5, 1).reshape(2560, 128), ACROSS)
    own_there = send(own, CORES)

    def edge(column):
        return jnp.concatenate([above[:, :, None, column], cells[:, :, :, column], below[:, :, None, column]], axis=2)

    left, right = send(edge(29), column_step(1)), send(edge(0), column_step(-1))
    shard, left, right, own_there = lax.optimization_barrier((jnp.stack(near), left, right, own_there))
    weights = [shard] + [send(shard, around_by_core(1, -by)) for by in (1, 2, 3)]
    own_rim, other_rim = pack_rims(position, above, below, left, right)
    across_rim = send(other_rim, ACROSS)
    across, across_rim, weights[2] = lax.optimization_barrier((across, across_rim, weights[2]))
    rims = [own_rim, send(own_rim, CORES), across_rim, send(across_rim, CORES)]
    mains = [own, own_there, across, send(across, CORES)]
    by_frame = [sum(row[i] * taps[i] for i in range(3) if row[i]) for row in TAPS]
    by_frame = jnp.stack(by_frame).reshape(6, 3, 3, 2, 8, 128)
    by_row = [sum(row[j] * by_frame[:, j] for j in range(3) if row[j]) for row in ROW_TAPS]
    taps = jnp.stack(by_row, axis=1).reshape(6, 12, 2, 8, 128)
    taps = taps * jnp.array([1.0, 0.5], F32)[None, None, :, None, None]

    kept, sent = run_block(position, pack_cells(position, mains, rims), weights, taps)
    total = kept + send(sent, CORES).astype(F32)
    return total[:, :, None, :, :30].astype(BF16)


def solution(mesh):
    return jax.shard_map(
        on_device,
        mesh=mesh,
        in_specs=(
            P(None, None, "tile", None, None, "ch"),
            P("tile", None, "ch"),
            P(None, None, None, None, "ch"),
            P("ch", "tile"),
        ),
        out_specs=P(None, "ch", "tile", None, None, None),
        check_vma=False,
    )
```
